128 devices in a mesh: gx: 16 (over z, y), gy: 8 (over x, core).
Axes of the slice: x: 4, y: 4, z: 4, core: 2. Of those that a mesh axis runs over, the one named last changes fastest.
Arguments:
- populations: float32 [19, 512, 6144], P(None, 'gy', 'gx'), may hold values from 0 to 0.5, as said below
- heights: int32 [2, 512, 1536], replicated, may hold values from 0 to 4
- wall_class: int32 [512, 1536], replicated, may hold values from 0 to 3
- wetting: float32 [4], replicated, may hold values from -0.3 to 0.3
- owner: int32 [8, 16, 6], replicated, may hold values from -1 to 15, as said below
Outputs:
- stepped: float32 [8, 64, 19, 32, 128], P('gy', 'gx')
The draws below stay inside these ranges and needn't reach their ends.
Inputs may be any that keep to these rules, and one draw needn't show every extreme that they name: `populations`: each population is w_i times a factor between 0.5 and 1.5. `owner`: each row of gy holds between 49 and 64 active blocks; in each row, every receiver gets at most 4 blocks and some receiver exactly 4; no device's blocks go twice to one receiver.
All inputs are finite; a program needn't handle non-finite values.
Results may differ from the reference program's by a relative error of at most 0.0003.
Values sent between devices are 32-bit elements; how exact they have to be, the bound alone decides.
No kernel may reach another device: no remote copies, remote signals or barrier semaphores. Data moves between devices by JAX's collectives and lax.ppermute only.
A program may use at most 128 MiB of HBM per device.

```python
import jax
import jax.numpy as jnp
import numpy as np

B = 32
CZ = 4
BXD = 3
BYD = 2
CAP = 4
NCLS = 4
BLK = 6
NX = 1536
NY = 512
N_GX = 16
N_GY = 8


LATTICE_WEIGHTS = [1.0 / 3.0] + [1.0 / 18.0] * 6 + [1.0 / 36.0] * 12


def drop_centre(key):
    return jax.random.randint(jax.random.fold_in(key, 7), (), 0, NX)


def draw_populations(key, part):
    key = jax.random.fold_in(key, 11)
    weights = jnp.asarray(LATTICE_WEIGHTS, jnp.float32)[:, None, None]
    factor = 1.0 + 0.3 * jax.random.uniform(key, (19, NY, NX * CZ), jnp.float32, -1.0, 1.0)
    return weights * factor


def draw_heights(key, part):
    centre = drop_centre(key)
    key = jax.random.fold_in(key, 13)
    first_key, second_key = jax.random.split(key, 2)
    across = jnp.arange(NX)
    offset = jnp.abs(across - centre)
    offset = jnp.minimum(offset, NX - offset)
    radius_cells = max(NX // 6, 1)
    profile = CZ + CZ // 4 - offset * offset * CZ // (radius_cells * radius_cells)
    jitter = jax.random.randint(first_key, (NY, NX), -(CZ // 4), 1)
    first = jnp.clip(profile[None, :] + jitter, 0, CZ)
    change = jax.random.randint(second_key, (NY, NX), -2, 3)
    second = jnp.clip(first + change, 0, CZ)
    return jnp.stack([first, second]).astype(jnp.int32)


def draw_owner(key, part):
    centre = drop_centre(key) // B
    key = jax.random.fold_in(key, 17)
    count_key, tie_key, perm_key = jax.random.split(key, 3)
    block_cols = N_GX * BXD
    blocks_row = N_GX * BLK
    number = jnp.arange(blocks_row)
    home_column = number // BLK
    local_index = number % BLK
    column = home_column * BXD + local_index % BXD
    offset = jnp.abs(column - centre)
    offset = jnp.minimum(offset, block_cols - offset)
    tie_break = jax.vmap(lambda row_key: jax.random.permutation(row_key, blocks_row))(jax.random.split(tie_key, N_GY))
    distance_score = offset[None, :] * blocks_row + tie_break
    sorted_order = jnp.argsort(distance_score, axis=1)
    position = jnp.argsort(sorted_order, axis=1)
    wanted = jax.random.randint(count_key, (N_GY, 1), 3 * N_GX + 1, 4 * N_GX + 1)
    active = (position < wanted).astype(jnp.int32)
    active_rank = jnp.cumsum(active, axis=1) - active
    receivers_perm = jax.vmap(lambda row_key: jax.random.permutation(row_key, N_GX))(jax.random.split(perm_key, N_GY))
    target = jnp.take_along_axis(receivers_perm, active_rank % N_GX, axis=1)
    owner = jnp.where(active > 0, target, -1)
    return owner.reshape(N_GY, N_GX, BLK).astype(jnp.int32)


def touch_ends(drawn, own_key, least, largest):
    shape = drawn.shape
    spot = [jax.random.randint(jax.random.fold_in(own_key, axis), (), 0, shape[axis]) for axis in range(len(shape))]
    drawn = drawn.at[tuple(spot)].set(least)
    longest = shape.index(max(shape))
    spot[longest] = (spot[longest] + 1) % shape[longest]
    return drawn.at[tuple(spot)].set(largest)


def setup_inputs(seed: int = 0) -> dict:
    key_list = jax.random.split(jax.random.key(seed), 6)
    populations = draw_populations(jax.random.fold_in(key_list[5], 71), 0)
    heights = draw_heights(jax.random.fold_in(key_list[5], 71), 0)
    wall_class = touch_ends(jax.random.randint(key_list[2], (NY, NX), 0, NCLS), jax.random.fold_in(key_list[2], 1), 0, NCLS - 1).astype(jnp.int32)
    wetting = jnp.clip(jax.random.uniform(key_list[3], (NCLS,), jnp.float32, -0.3, 0.3), -0.3, 0.3)
    owner = draw_owner(jax.random.fold_in(key_list[5], 71), 0)
    return {"populations": populations, "heights": heights, "wall_class": wall_class, "wetting": wetting, "owner": owner}


VELOCITY = np.array([[0, 0, 0], [1, 0, 0], [-1, 0, 0], [0, 1, 0], [0, -1, 0], [0, 0, 1], [0, 0, -1],
                     [1, 1, 0], [-1, -1, 0], [1, -1, 0], [-1, 1, 0], [1, 0, 1], [-1, 0, -1], [1, 0, -1],
                     [-1, 0, 1], [0, 1, 1], [0, -1, -1], [0, 1, -1], [0, -1, 1]])
LATTICE_WEIGHTS = [1.0 / 3.0] + [1.0 / 18.0] * 6 + [1.0 / 36.0] * 12
OPPOSITE = [0, 2, 1, 4, 3, 6, 5, 8, 7, 10, 9, 12, 11, 14, 13, 16, 15, 18, 17]
OMEGA_EVEN = 1.6
OMEGA_ODD = 0.5


def collide(populations, gas_density):
    planes = [populations[..., number, :, :, :] for number in range(19)]
    density = sum(planes)
    velocity = []
    for axis_number in range(3):
        momentum = jnp.zeros_like(density)
        for number in range(19):
            factor = int(VELOCITY[number, axis_number])
            if factor != 0:
                momentum = momentum + float(factor) * planes[number]
        velocity.append(momentum / density)
    square = velocity[0] * velocity[0] + velocity[1] * velocity[1] + velocity[2] * velocity[2]
    equilibrium = []
    for number in range(19):
        projection = jnp.zeros_like(density)
        for axis_number in range(3):
            factor = int(VELOCITY[number, axis_number])
            if factor != 0:
                projection = projection + float(factor) * velocity[axis_number]
        equilibrium.append(LATTICE_WEIGHTS[number] * density * (1.0 + 3.0 * projection + 4.5 * projection * projection - 1.5 * square))
    results = []
    for number in range(19):
        partner = OPPOSITE[number]
        even_part = 0.5 * (planes[number] + planes[partner]) - 0.5 * (equilibrium[number] + equilibrium[partner])
        odd_part = 0.5 * (planes[number] - planes[partner]) - 0.5 * (equilibrium[number] - equilibrium[partner])
        relaxed = planes[number] - OMEGA_EVEN * even_part - OMEGA_ODD * odd_part
        results.append(jnp.where(gas_density > 0, LATTICE_WEIGHTS[number] * gas_density, relaxed))
    return jnp.stack(results, axis=-4)


def stream(padded):
    out_rows = padded.shape[-3] - 2
    out_cols = padded.shape[-2] - 2
    results = []
    for number in range(19):
        step_x = int(VELOCITY[number, 0])
        step_y = int(VELOCITY[number, 1])
        step_z = int(VELOCITY[number, 2])
        shifted = padded[..., number, 1 - step_y:1 - step_y + out_rows, 1 - step_x:1 - step_x + out_cols, :]
        if step_z == 1:
            bounce = padded[..., OPPOSITE[number], 1:1 + out_rows, 1:1 + out_cols, 0:1]
            shifted = jnp.concatenate([bounce, shifted[..., :-1]], axis=-1)
        elif step_z == -1:
            inflow = jnp.full(shifted[..., :1].shape, LATTICE_WEIGHTS[number], jnp.float32)
            shifted = jnp.concatenate([shifted[..., 1:], inflow], axis=-1)
        results.append(shifted)
    return jnp.stack(results, axis=-4)


def column_fields(owner, wall_class, wetting):
    grid_rows = owner.shape[0]
    grid_cols = owner.shape[1]
    active = owner >= 0
    block_grid = active.reshape(grid_rows, grid_cols, BYD, BXD).transpose(0, 2, 1, 3).reshape(grid_rows * BYD, grid_cols * BXD)
    active_cells = jnp.repeat(jnp.repeat(block_grid, B, axis=0), B, axis=1)
    matches = wall_class[..., None] == jnp.arange(NCLS)
    gas_level = 1.0 + jnp.sum(jnp.where(matches, wetting, 0.0), axis=-1)
    return active_cells, gas_level


def gas_fields(first_heights, second_heights, active_cells, gas_level, depth_count):
    depth_index = jnp.arange(depth_count)
    fields = []
    for column_heights in (first_heights, second_heights):
        is_fluid = active_cells[..., None] & (depth_index < column_heights[..., None])
        fields.append(jnp.where(is_fluid, 0.0, gas_level[..., None]))
    return fields


def reference(populations, heights, wall_class, wetting, owner):
    active_cells, gas_level = column_fields(owner, wall_class, wetting)
    gas_one, gas_two = gas_fields(heights[0], heights[1], active_cells, gas_level, CZ)
    current = populations.reshape(19, NY, NX, CZ)
    for gas_density in (gas_one, gas_two):
        posted = collide(current, gas_density)
        padded = jnp.pad(posted, ((0, 0), (1, 1), (1, 1), (0, 0)), mode="wrap")
        current = stream(padded)
    flat_owner = owner.reshape(N_GY, N_GX * BLK)
    receivers = (flat_owner[..., None] == jnp.arange(N_GX)).astype(jnp.int32)
    earlier = jnp.cumsum(receivers, axis=1) - receivers
    slot_of = jnp.sum(earlier * receivers, axis=-1)
    target = jnp.where(flat_owner >= 0, flat_owner * CAP + slot_of, N_GX * CAP)
    blocks = current.reshape(19, N_GY, BYD, B, N_GX, BXD, B, CZ).transpose(1, 4, 2, 5, 0, 3, 6, 7)
    blocks = blocks.reshape(N_GY, N_GX * BLK, 19, B, B * CZ)
    stepped = jnp.zeros((N_GY, N_GX * CAP + 1, 19, B, B * CZ), jnp.float32)
    row_numbers = jnp.arange(N_GY)[:, None] + 0 * target
    stepped = stepped.at[row_numbers, target].set(blocks)
    return stepped[:, :N_GX * CAP]
```

```python
import functools

import jax
import jax.numpy as jnp
import numpy as np
from jax import lax
from jax.experimental import pallas as pl
from jax.experimental.pallas import tpu as pltpu
from jax.sharding import PartitionSpec as P

B = 32
CZ = 4
BXD = 3
BYD = 2
CAP = 4
BLK = BXD * BYD
Q = 19
TILE = 8
LANES = 128
ROWS = 64
GROUPS = ROWS // TILE
SENT = [i for i in range(Q) if i != 17]
TAIL = 17
NDEV = 16
PIECE = BLK * (B + 4)
SLOTS = CAP * (B + 4)
BASE = 16
PADDED = ROWS + 2 * BASE

VELOCITY = [
    (0, 0, 0),
    (1, 0, 0),
    (-1, 0, 0),
    (0, 1, 0),
    (0, -1, 0),
    (0, 0, 1),
    (0, 0, -1),
    (1, 1, 0),
    (-1, -1, 0),
    (1, -1, 0),
    (-1, 1, 0),
    (1, 0, 1),
    (-1, 0, -1),
    (1, 0, -1),
    (-1, 0, 1),
    (0, 1, 1),
    (0, -1, -1),
    (0, 1, -1),
    (0, -1, 1),
]
WEIGHTS = [1.0 / 3.0] + [1.0 / 18.0] * 6 + [1.0 / 36.0] * 12
OPPOSITE = [0, 2, 1, 4, 3, 6, 5, 8, 7, 10, 9, 12, 11, 14, 13, 16, 15, 18, 17]
CARRIERS = (6, 12, 13)
FIXED_TOP = (6, 12, 13, 16)

f32 = jnp.float32
i32 = jnp.int32
VMEM_LIMIT = 32 * 1024 * 1024


def params(**more):
    return pltpu.CompilerParams(vmem_limit_bytes=VMEM_LIMIT, **more)


def lane_of():
    return lax.broadcasted_iota(i32, (TILE, LANES), 1)


def row_of():
    return lax.broadcasted_iota(i32, (TILE, LANES), 0)


def collide(f, gas):
    pairs = [(i, i + 1) for i in range(1, Q, 2)]
    total = {i: f[i] + f[o] for i, o in pairs}
    diff = {i: f[i] - f[o] for i, o in pairs}
    rho = f[0]
    for i, _ in pairs:
        rho = rho + total[i]
    jx = diff[1] + diff[7] + diff[9] + diff[11] + diff[13]
    jy = diff[3] + diff[7] - diff[9] + diff[15] + diff[17]
    jz = diff[5] + diff[11] - diff[13] + diff[15] - diff[17]
    inv = 1.0 / rho
    scaled = rho - 1.5 * inv * (jx * jx + jy * jy + jz * jz)
    along = {
        1: jx,
        3: jy,
        5: jz,
        7: jx + jy,
        9: jx - jy,
        11: jx + jz,
        13: jx - jz,
        15: jy + jz,
        17: jy - jz,
    }
    is_gas = gas > 0
    out = [None] * Q
    out[0] = jnp.where(
        is_gas, WEIGHTS[0] * gas, -0.6 * f[0] + (1.6 * WEIGHTS[0]) * scaled
    )
    for first, last in ((1, 5), (7, 17)):
        w = WEIGHTS[first]
        base = (1.6 * w) * scaled
        bend = (7.2 * w) * inv
        held = w * gas
        for i in range(first, last + 1, 2):
            cj = along[i]
            even = base + bend * (cj * cj) - 0.3 * total[i]
            odd = 0.25 * diff[i] + (1.5 * w) * cj
            out[i] = jnp.where(is_gas, held, even + odd)
            out[i + 1] = jnp.where(is_gas, held, even - odd)
    return out


def shifted(load, c, shift, lane):
    if shift == 0:
        return load(c)
    if shift > 0:
        here = load(c)
        if c > 0:
            here = jnp.where(lane >= LANES - shift, load(c - 1), here)
        return pltpu.roll(here, shift, 1)
    here = load(c)
    if c < 3:
        here = jnp.where(lane < -shift, load(c + 1), here)
    return pltpu.roll(here, LANES + shift, 1)


def pull(load, i, c, lane, extra):
    cx, cy, cz = VELOCITY[i]
    moved = shifted(lambda t: load(i, t, cy), c, 4 * cx + cz - extra, lane)
    if cz == 1:
        wall = shifted(lambda t: load(OPPOSITE[i], t, 0), c, -extra, lane)
        moved = jnp.where(lane % CZ == 0, wall, moved)
    elif cz == -1:
        moved = jnp.where(lane % CZ == CZ - 1, jnp.float32(WEIGHTS[i]), moved)
    return moved


def pack_rows_kernel(first_ref, last_ref, up_ref, down_ref):
    for i in range(Q):
        up_ref[2 * i : 2 * i + 2, :] = first_ref[i, 0:2, :]
        down_ref[2 * i : 2 * i + 2, :] = last_ref[i, TILE - 2 : TILE, :]


def pack_rows(populations):
    width = populations.shape[2]
    out = jax.ShapeDtypeStruct((2 * Q + 2, width), f32)
    return pl.pallas_call(
        pack_rows_kernel,
        grid=(1,),
        in_specs=[
            pl.BlockSpec((Q, TILE, width), lambda g: (0, 0, 0)),
            pl.BlockSpec((Q, TILE, width), lambda g: (0, GROUPS - 1, 0)),
        ],
        out_specs=[pl.BlockSpec((2 * Q + 2, width), lambda g: (0, 0))] * 2,
        out_shape=[out, out],
        compiler_params=params(),
        name="pack_rows",
    )(populations, populations)


def pack_cols_kernel(pop_ref, below_ref, above_ref, out_ref, halo_ref):
    lane = lane_of()
    for i in range(Q):
        packed = pop_ref[i, 0:TILE, :]
        for g in range(1, GROUPS):
            rolled = pltpu.roll(pop_ref[i, TILE * g : TILE * (g + 1), :], 16 * g, 1)
            packed = jnp.where(lane >= 16 * g, rolled, packed)
        out_ref[i] = packed
    halo_ref[...] = jnp.zeros(halo_ref.shape, f32)
    for i in range(Q):
        halo_ref[i, 0:2, :] = below_ref[2 * i : 2 * i + 2, :]
        halo_ref[i, TILE - 2 : TILE, :] = above_ref[2 * i : 2 * i + 2, :]
    for part in range(3):
        packed = halo_ref[8 * part]
        for g in range(1, 8):
            if 8 * part + g < Q:
                rolled = pltpu.roll(halo_ref[8 * part + g], 16 * g, 1)
                packed = jnp.where(lane >= 16 * g, rolled, packed)
        out_ref[Q + part] = packed


def pack_cols(populations, below, above):
    return pl.pallas_call(
        pack_cols_kernel,
        grid=(1,),
        in_specs=[
            pl.BlockSpec((Q, ROWS, LANES), lambda g: (0, 0, 0)),
            pl.BlockSpec((2 * Q + 2, LANES), lambda g: (0, 0)),
            pl.BlockSpec((2 * Q + 2, LANES), lambda g: (0, 0)),
        ],
        out_specs=pl.BlockSpec((Q + 3, TILE, LANES), lambda g: (0, 0, 0)),
        out_shape=jax.ShapeDtypeStruct((Q + 3, TILE, LANES), f32),
        scratch_shapes=[pltpu.VMEM((Q, TILE, LANES), f32)],
        compiler_params=params(),
        name="pack_cols",
    )(populations, below, above)


def own_kernel(
    pos_ref,
    owner_ref,
    wet_ref,
    pop_ref,
    h0_ref,
    h1_ref,
    ht0_ref,
    ht1_ref,
    hb0_ref,
    hb1_ref,
    k0_ref,
    k1_ref,
    kt0_ref,
    kt1_ref,
    kb0_ref,
    kb1_ref,
    post_ref,
    gas_ref,
    packed_ref,
):
    gy, gx = (pos_ref[0], pos_ref[1])
    offset = (gx * (BXD * B)) % LANES
    wide = 4 * LANES
    cell = lax.broadcasted_iota(i32, (2 * LANES, wide), 0)
    place = lax.broadcasted_iota(i32, (2 * LANES, wide), 1)
    spread = (cell == offset + place // CZ).astype(f32)

    def widen(left, right):
        both = jnp.concatenate([left, right], axis=1).astype(f32)
        return jnp.dot(both, spread, preferred_element_type=f32)

    def active(row, col, j):
        return (owner_ref[(row * NDEV + col) * BLK + j] >= 0).astype(f32)

    next_gx = (gx + 1) % NDEV

    def act_tile(row, by, c):
        return active(row, gx, BXD * by + c) if c < BXD else active(row, next_gx, BXD * by)

    def level_of(kind):
        value = wet_ref[0]
        value = jnp.where(kind > 0.5, wet_ref[1], value)
        value = jnp.where(kind > 1.5, wet_ref[2], value)
        value = jnp.where(kind > 2.5, wet_ref[3], value)
        return 1.0 + value

    level = level_of(widen(k0_ref[...], k1_ref[...]))
    sub16 = lax.broadcasted_iota(i32, (TILE, LANES), 0) < 4
    kind_halo = jnp.where(sub16, kb0_ref[...], kt0_ref[...])
    kind_halo1 = jnp.where(sub16, kb1_ref[...], kt1_ref[...])
    level_halo = level_of(widen(kind_halo, kind_halo1))
    depth = (lane_of() % CZ).astype(f32)
    up_gy, down_gy = ((gy + 7) % 8, (gy + 1) % 8)
    lane = lane_of()
    for s in range(2):
        tall = widen(h0_ref[s], h1_ref[s])
        for c in range(4):
            for by in range(BYD):
                act = act_tile(gy, by, c)
                for rr in range(4):
                    g = 4 * by + rr
                    height = tall[TILE * g : TILE * (g + 1), LANES * c : LANES * (c + 1)]
                    here = level[TILE * g : TILE * (g + 1), LANES * c : LANES * (c + 1)]
                    gas_ref[s, g, c] = jnp.where(depth < height * act, 0.0, here)
        halo = widen(
            jnp.where(sub16, hb0_ref[s], ht0_ref[s]), jnp.where(sub16, hb1_ref[s], ht1_ref[s])
        )
        for c in range(4):
            act = jnp.where(sub16, act_tile(down_gy, 0, c), act_tile(up_gy, 1, c))
            height = halo[:, LANES * c : LANES * (c + 1)]
            here = level_halo[:, LANES * c : LANES * (c + 1)]
            gas_ref[s, GROUPS, c] = jnp.where(depth < height * act, 0.0, here)
    packed = gas_ref[0, 0, 3]
    for g in range(1, GROUPS):
        packed = jnp.where(lane >= 16 * g, pltpu.roll(gas_ref[0, g, 3], 16 * g, 1), packed)
    packed_ref[...] = packed

    def step(g, carry):
        rows = pl.ds(pl.multiple_of(TILE * g, TILE), TILE)
        for c in range(3):
            f = [pop_ref[i, rows, LANES * c : LANES * (c + 1)] for i in range(Q)]
            out = collide(f, gas_ref[0, g, c])
            for i in range(Q):
                post_ref[i, c, rows, :] = out[i]
        return carry

    lax.fori_loop(0, GROUPS, step, 0)


def own_part(pos, owner, wetting, populations, heights, wall_class):
    n_y = heights.shape[1] // TILE
    n_x = heights.shape[2] // LANES

    def first_tile(pos):
        return (pos[1] * (BXD * B)) // LANES

    def second_tile(pos):
        return (first_tile(pos) + 1) % n_x

    def rows_above(pos):
        return (pos[0] * GROUPS + n_y - 1) % n_y

    def rows_below(pos):
        return (pos[0] * GROUPS + GROUPS) % n_y

    h_specs, k_specs = ([], [])
    for count, row in (
        (ROWS, lambda pos: pos[0]),
        (TILE, rows_above),
        (TILE, rows_below),
    ):
        for col in (first_tile, second_tile):
            h_specs.append(
                pl.BlockSpec(
                    (2, count, LANES), lambda g, pos, row=row, col=col: (0, row(pos), col(pos))
                )
            )
            k_specs.append(
                pl.BlockSpec(
                    (count, LANES), lambda g, pos, row=row, col=col: (row(pos), col(pos))
                )
            )
    smem = pl.BlockSpec(memory_space=pltpu.SMEM)
    return pl.pallas_call(
        own_kernel,
        grid_spec=pltpu.PrefetchScalarGridSpec(
            num_scalar_prefetch=1,
            grid=(1,),
            in_specs=[smem, smem, pl.BlockSpec((Q, ROWS, 3 * LANES), lambda g, pos: (0, 0, 0))]
            + h_specs
            + k_specs,
            out_specs=[
                pl.BlockSpec((Q, 3, ROWS, LANES), lambda g, pos: (0, 0, 0, 0)),
                pl.BlockSpec((2, GROUPS + 1, 4, TILE, LANES), lambda g, pos: (0, 0, 0, 0, 0)),
                pl.BlockSpec((TILE, LANES), lambda g, pos: (0, 0)),
            ],
        ),
        out_shape=[
            jax.ShapeDtypeStruct((Q, 3, ROWS, LANES), f32),
            jax.ShapeDtypeStruct((2, GROUPS + 1, 4, TILE, LANES), f32),
            jax.ShapeDtypeStruct((TILE, LANES), f32),
        ],
        compiler_params=params(),
        cost_estimate=pl.CostEstimate(flops=8_000_000, bytes_accessed=5_000_000, transcendentals=0),
        name="own_cells",
    )(pos, owner, wetting, populations, *([heights] * 6), *([wall_class] * 6))


def steps_kernel(own_ref, gas_ref, packed_ref, below_ref, above_ref, right_ref, out_ref, one, two, halo, sem):
    copy = pltpu.make_async_copy(own_ref, one.at[:, 0:3, pl.ds(BASE, ROWS), :], sem)
    copy.start()
    lane = lane_of()
    sub_low = row_of() < 4

    def keep_halo(ref, c, out):
        for i in range(Q):
            ref[i, c, BASE + ROWS : BASE + ROWS + TILE, :] = out[i]
            ref[i, c, BASE - TILE : BASE, :] = out[i]

    out = collide([right_ref[i] for i in range(Q)], packed_ref[...])
    for i in range(Q):
        for g in range(GROUPS):
            tile = out[i] if g == 0 else pltpu.roll(out[i], LANES - 16 * g, 1)
            one[i, 3, BASE + TILE * g : BASE + TILE * (g + 1), :] = tile
    corner = []
    for i in range(Q):
        tile, g = (right_ref[Q + i // 8], i % 8)
        corner.append(tile if g == 0 else pltpu.roll(tile, LANES - 16 * g, 1))
    keep_halo(one, 3, collide(corner, gas_ref[0, GROUPS, 3]))
    halo[...] = jnp.ones(halo.shape, f32)
    for i in range(Q):
        for c in range(3):
            cols = slice(LANES * c, LANES * (c + 1))
            halo[i, c, 0:2, :] = below_ref[2 * i : 2 * i + 2, cols]
            halo[i, c, TILE - 2 : TILE, :] = above_ref[2 * i : 2 * i + 2, cols]

    def halo_step(c, carry):
        out = collide([halo[i, c] for i in range(Q)], gas_ref[0, GROUPS, c])
        keep_halo(one, c, out)
        return carry

    lax.fori_loop(0, 3, halo_step, 0)
    copy.wait()

    def second(g, carry):
        def load(i, c, dy):
            return one[i, c, pl.ds(TILE * g + (BASE - dy), TILE), :]

        for c in range(4):
            out = collide([pull(load, i, c, lane, 0) for i in range(Q)], gas_ref[1, g, c])
            for i in range(Q):
                two[i, c, pl.ds(pl.multiple_of(TILE * g + BASE, TILE), TILE), :] = out[i]
        return carry

    lax.fori_loop(0, GROUPS, second, 0)

    def load_edges(i, c, dy):
        low = BASE + ROWS - dy
        high = BASE - TILE - dy
        return jnp.where(sub_low, one[i, c, low : low + TILE, :], one[i, c, high : high + TILE, :])

    for c in range(4):
        keep_halo(
            two,
            c,
            collide([pull(load_edges, i, c, lane, 0) for i in range(Q)], gas_ref[1, GROUPS, c]),
        )

    for by in range(BYD):

        def last(rr, carry):
            g = 4 * by + rr

            def load(i, c, dy):
                return two[i, c, pl.ds(TILE * g + (BASE - dy), TILE), :]

            for c in range(3):
                j = BXD * by + c
                tail = pull(load, TAIL, c, lane, 8)
                for n, i in enumerate(SENT):
                    value = pull(load, i, c, lane, 8)
                    if i in CARRIERS:
                        back = 3 - CARRIERS.index(i)
                        value = jnp.where(lane % CZ == CZ - 1, pltpu.roll(tail, back, 1), value)
                    if n < NDEV:
                        out_ref[n, pl.ds(pl.multiple_of(B * j + TILE * rr, TILE), TILE), :] = value
                    else:
                        m = 8 * (n - NDEV) + 2 * rr
                        at = BLK * B + 4 * j
                        out_ref[m, at : at + 4, :] = value[0:4]
                        out_ref[m + 1, at : at + 4, :] = value[4:8]
            return carry

        lax.fori_loop(0, 4, last, 0)


def steps(own, gas, packed, below, above, right):
    vmem = pl.BlockSpec(memory_space=pltpu.VMEM)
    return pl.pallas_call(
        steps_kernel,
        in_specs=[pl.BlockSpec(memory_space=pl.ANY)] + [vmem] * 5,
        out_specs=vmem,
        out_shape=jax.ShapeDtypeStruct((NDEV, PIECE, LANES), f32),
        scratch_shapes=[
            pltpu.VMEM((Q, 4, PADDED, LANES), f32),
            pltpu.VMEM((Q, 4, PADDED, LANES), f32),
            pltpu.VMEM((Q, 3, TILE, LANES), f32),
            pltpu.SemaphoreType.DMA,
        ],
        compiler_params=params(),
        cost_estimate=pl.CostEstimate(flops=20_000_000, bytes_accessed=6_000_000, transcendentals=0),
        name="two_steps",
    )(own, gas, packed, below, above, right)


def sort_kernel(table_ref, in_ref, out_ref):
    lane = lane_of()
    sub_low = row_of() < 4

    def source(entry):
        block = jnp.maximum(entry, 0)
        s = block // BLK
        j = block - s * BLK
        first = (j == 0) | (j == BXD)
        before_s = jnp.where(first, jnp.where(s == 0, NDEV - 1, s - 1), s)
        before_j = jnp.where(first, j + BXD - 1, j - 1)
        return (s, j, before_s, before_j)

    def receiver(d, carry):
        halves = []
        for k in range(CAP):
            entry = table_ref[d * CAP + k]
            valid = entry >= 0
            s, j, ps, pj = source(entry)
            for t in range(4):
                now = in_ref[s, pl.ds(pl.multiple_of(B * j + TILE * t, TILE), TILE), :]
                before = in_ref[ps, pl.ds(pl.multiple_of(B * pj + TILE * t, TILE), TILE), :]
                tile = pltpu.roll(jnp.where(lane >= 120, before, now), 8, 1)
                out_ref[d, B * k + TILE * t : B * k + TILE * (t + 1), :] = jnp.where(valid, tile, 0.0)

            def half(s, j):
                pair = j // 2
                tile = in_ref[s, pl.ds(pl.multiple_of(BLK * B + TILE * pair, TILE), TILE), :]
                return jnp.where(j - 2 * pair == k % 2, tile, pltpu.roll(tile, 4, 0))

            tile = pltpu.roll(jnp.where(lane >= 120, half(ps, pj), half(s, j)), 8, 1)
            halves.append(jnp.where(valid, tile, 0.0))
        for pair in range(CAP // 2):
            at = CAP * B + TILE * pair
            out_ref[d, at : at + TILE, :] = jnp.where(sub_low, halves[2 * pair], halves[2 * pair + 1])
        return carry

    lax.fori_loop(0, NDEV, receiver, 0)


def sort_blocks(table, arrived):
    vmem = pl.BlockSpec(memory_space=pltpu.VMEM)
    return pl.pallas_call(
        sort_kernel,
        in_specs=[pl.BlockSpec(memory_space=pltpu.SMEM), vmem],
        out_specs=vmem,
        out_shape=jax.ShapeDtypeStruct((NDEV, SLOTS, LANES), f32),
        compiler_params=params(),
        name="sort_blocks",
    )(table, arrived)


def restore_kernel(taken_ref, in_ref, out_ref):
    lane = lane_of()
    sub_low = row_of() < 4
    top = lane % CZ == CZ - 1
    place = lane % CZ

    def slot(k, taken, t):
        rows = slice(B * k + TILE * t, B * k + TILE * (t + 1))
        planes = {m: in_ref[m, rows, :] for m in range(NDEV)}
        pair = CAP * B + TILE * (k // 2)
        for p in range(2):
            a = in_ref[8 * p + 2 * t, pair : pair + TILE, :]
            b = in_ref[8 * p + 2 * t + 1, pair : pair + TILE, :]
            if k % 2 == 0:
                b = pltpu.roll(b, 4, 0)
            else:
                a = pltpu.roll(a, 4, 0)
            planes[NDEV + p] = jnp.where(sub_low, a, b)
        at = slice(TILE * t, TILE * (t + 1))
        last = taken * jnp.float32(WEIGHTS[TAIL])
        parts = [pltpu.roll(planes[i], LANES - 3 + n, 1) for n, i in enumerate(CARRIERS)]
        tail = jnp.where(place == 0, parts[0], jnp.where(place == 1, parts[1], parts[2]))
        out_ref[0, k, TAIL, at, :] = jnp.where(top, last, tail)
        for n, i in enumerate(SENT):
            value = planes[n]
            if i in FIXED_TOP:
                value = jnp.where(top, taken * jnp.float32(WEIGHTS[i]), value)
            out_ref[0, k, i, at, :] = value

    for k in range(CAP):
        taken = (taken_ref[0] > k).astype(f32)
        for t in range(4):
            slot(k, taken, t)


def restore(taken, arrived):
    vmem = pl.BlockSpec(memory_space=pltpu.VMEM)
    return pl.pallas_call(
        restore_kernel,
        in_specs=[pl.BlockSpec(memory_space=pltpu.SMEM), vmem],
        out_specs=vmem,
        out_shape=jax.ShapeDtypeStruct((1, CAP, Q, B, LANES), f32),
        compiler_params=params(),
        name="restore",
    )(taken, arrived)


def tables(owner, gy, gx):
    flat = lax.dynamic_index_in_dim(owner, gy, 0, keepdims=False).reshape(-1)
    number = jnp.arange(NDEV * BLK)
    same = (flat[:, None] == flat[None, :]) & (number[None, :] < number[:, None])
    slot = jnp.sum(same.astype(i32), axis=1)
    target = jnp.where(flat >= 0, flat * CAP + slot, -1)
    hit = target[:, None] == jnp.arange(NDEV * CAP)[None, :]
    table = jnp.max(jnp.where(hit, number[:, None], -1), axis=0).astype(i32)
    taken = jnp.sum((flat == gx).astype(i32)).reshape(1)
    return (table, taken)


def local(populations, heights, wall_class, wetting, owner):
    gy = lax.axis_index("gy")
    gx = lax.axis_index("gx")
    n_gy = lax.axis_size("gy")
    pos = jnp.stack([gy, gx]).astype(i32)
    up, down = pack_rows(populations)
    below = lax.ppermute(up, "gy", [(i, (i - 1) % n_gy) for i in range(n_gy)])
    above = lax.ppermute(down, "gy", [(i, (i + 1) % n_gy) for i in range(n_gy)])
    message = pack_cols(populations, below, above)
    right = lax.ppermute(message, "gx", [(i, (i - 1) % NDEV) for i in range(NDEV)])
    own, gas, packed = own_part(pos, owner.reshape(-1), wetting, populations, heights, wall_class)
    table, taken = tables(owner, gy, gx)
    spread = steps(own, gas, packed, below, above, right)
    gathered = lax.all_to_all(spread, "gx", split_axis=0, concat_axis=0, tiled=True)
    chosen = sort_blocks(table, gathered)
    arrived = lax.all_to_all(chosen, "gx", split_axis=0, concat_axis=0, tiled=True)
    return restore(taken, arrived)


def solution(mesh):
    return jax.shard_map(
        local,
        mesh=mesh,
        in_specs=(P(None, "gy", "gx"), P(), P(), P(), P()),
        out_specs=P("gy", "gx", None, None, None),
        check_vma=False,
    )
```

```python
import functools

import jax
import jax.numpy as jnp
import numpy as np
from jax import lax
from jax.experimental import pallas as pl
from jax.experimental.pallas import tpu as pltpu
from jax.sharding import PartitionSpec as P

B = 32
CZ = 4
BXD = 3
BYD = 2
CAP = 4
NCLS = 4
BLK = BXD * BYD
Q = 19
TILE = 8
LANES = 128
ROWS = 64
GROUPS = ROWS // TILE
SENT = [i for i in range(Q) if i != 17]
TAIL = 17
NDEV = 16
PIECE = BLK * (B + 4)
SLOTS = CAP * (B + 4)

VELOCITY = [
    (0, 0, 0),
    (1, 0, 0),
    (-1, 0, 0),
    (0, 1, 0),
    (0, -1, 0),
    (0, 0, 1),
    (0, 0, -1),
    (1, 1, 0),
    (-1, -1, 0),
    (1, -1, 0),
    (-1, 1, 0),
    (1, 0, 1),
    (-1, 0, -1),
    (1, 0, -1),
    (-1, 0, 1),
    (0, 1, 1),
    (0, -1, -1),
    (0, 1, -1),
    (0, -1, 1),
]
WEIGHTS = [1.0 / 3.0] + [1.0 / 18.0] * 6 + [1.0 / 36.0] * 12
OPPOSITE = [0, 2, 1, 4, 3, 6, 5, 8, 7, 10, 9, 12, 11, 14, 13, 16, 15, 18, 17]
CARRIERS = (6, 12, 13)
FIXED_TOP = (6, 12, 13, 16)

f32 = jnp.float32
i32 = jnp.int32
MIB = 1024 * 1024


def params(limit=16 * MIB):
    return pltpu.CompilerParams(vmem_limit_bytes=limit)


VMEM_SPEC = pl.BlockSpec(memory_space=pltpu.VMEM)
HBM_SPEC = pl.BlockSpec(memory_space=pltpu.HBM)
SMEM_SPEC = pl.BlockSpec(memory_space=pltpu.SMEM)
OWN_SHAPE = jax.ShapeDtypeStruct((Q, 3, ROWS, LANES), f32)
TWO_SHAPE = jax.ShapeDtypeStruct((Q, 4, ROWS, LANES), f32)
RIGHT_SHAPE = jax.ShapeDtypeStruct((Q, ROWS, LANES), f32)
EDGE_SHAPE = jax.ShapeDtypeStruct((2 * Q + 2, 4 * LANES), f32)
MESSAGE_SHAPE = jax.ShapeDtypeStruct((NDEV, PIECE, LANES), f32)
HALVES_SHAPE = jax.ShapeDtypeStruct((NDEV, 4 * BLK, LANES), f32)


def lane_of():
    return lax.broadcasted_iota(i32, (TILE, LANES), 1)


def row_of():
    return lax.broadcasted_iota(i32, (TILE, LANES), 0)


def collide(f, gas):
    pairs = [(i, i + 1) for i in range(1, Q, 2)]
    total = {i: f[i] + f[o] for i, o in pairs}
    diff = {i: f[i] - f[o] for i, o in pairs}
    rho = f[0]
    for i, _ in pairs:
        rho = rho + total[i]
    jx = diff[1] + diff[7] + diff[9] + diff[11] + diff[13]
    jy = diff[3] + diff[7] - diff[9] + diff[15] + diff[17]
    jz = diff[5] + diff[11] - diff[13] + diff[15] - diff[17]
    inv = 1.0 / rho
    scaled = rho - 1.5 * inv * (jx * jx + jy * jy + jz * jz)
    along = {
        1: jx,
        3: jy,
        5: jz,
        7: jx + jy,
        9: jx - jy,
        11: jx + jz,
        13: jx - jz,
        15: jy + jz,
        17: jy - jz,
    }
    is_gas = gas > 0
    out = [None] * Q
    out[0] = jnp.where(
        is_gas, WEIGHTS[0] * gas, -0.6 * f[0] + (1.6 * WEIGHTS[0]) * scaled
    )
    for first, last in ((1, 5), (7, 17)):
        w = WEIGHTS[first]
        base = (1.6 * w) * scaled
        bend = (7.2 * w) * inv
        held = w * gas
        for i in range(first, last + 1, 2):
            cj = along[i]
            even = base + bend * (cj * cj) - 0.3 * total[i]
            odd = 0.25 * diff[i] + (1.5 * w) * cj
            out[i] = jnp.where(is_gas, held, even + odd)
            out[i + 1] = jnp.where(is_gas, held, even - odd)
    return out


def shifted(load, c, shift, lane):
    if shift == 0:
        return load(c)
    if shift > 0:
        here = load(c)
        if c > 0:
            here = jnp.where(lane >= LANES - shift, load(c - 1), here)
        return pltpu.roll(here, shift, 1)
    here = load(c)
    if c < 3:
        here = jnp.where(lane < -shift, load(c + 1), here)
    return pltpu.roll(here, LANES + shift, 1)


def pull(load, i, c, lane, extra):
    cx, cy, cz = VELOCITY[i]
    moved = shifted(lambda t: load(i, t, cy), c, 4 * cx + cz - extra, lane)
    if cz == 1:
        wall = shifted(lambda t: load(OPPOSITE[i], t, 0), c, -extra, lane)
        moved = jnp.where(lane % CZ == 0, wall, moved)
    elif cz == -1:
        moved = jnp.where(lane % CZ == CZ - 1, jnp.float32(WEIGHTS[i]), moved)
    return moved


def pack_cols_kernel(pop_ref, out_ref, buf, sem):
    copies = []
    for g in range(GROUPS):
        rows = pl.ds(TILE * g, TILE)
        copies.append(
            pltpu.make_async_copy(
                pop_ref.at[:, rows, pl.ds(0, LANES)], buf.at[:, rows, :], sem.at[g]
            )
        )
        copies[-1].start()
    for copy in copies:
        copy.wait()
    lane = lane_of()
    for i in range(Q):
        packed = buf[i, 0:TILE, :]
        for g in range(1, GROUPS):
            rolled = pltpu.roll(buf[i, TILE * g : TILE * (g + 1), :], 16 * g, 1)
            packed = jnp.where(lane >= 16 * g, rolled, packed)
        out_ref[i] = packed


def pack_cols(populations):
    return pl.pallas_call(
        pack_cols_kernel,
        in_specs=[HBM_SPEC],
        out_specs=VMEM_SPEC,
        out_shape=jax.ShapeDtypeStruct((Q, TILE, LANES), f32),
        scratch_shapes=[pltpu.VMEM((Q, ROWS, LANES), f32), pltpu.SemaphoreType.DMA((GROUPS,))],
        compiler_params=params(63 * MIB),
        name="pack_cols",
    )(populations)


def own_kernel(
    owner_ref,
    wet_ref,
    pop_hbm,
    height_hbm,
    kind_hbm,
    post_ref,
    gas_ref,
    packed_ref,
    up_ref,
    down_ref,
    pop,
    height,
    kind,
    pop_sem,
    field_sem,
):
    gy, gx = (lax.axis_index("gy"), lax.axis_index("gx"))
    n_gy = height_hbm.shape[1] // ROWS
    n_x = height_hbm.shape[2] // LANES
    first = (gx * (BXD * B)) // LANES
    offset = gx * (BXD * B) - first * LANES
    second = lax.rem(first + 1, n_x)
    up_gy, down_gy = (lax.rem(gy + n_gy - 1, n_gy), lax.rem(gy + 1, n_gy))
    copies = []
    for half, col in enumerate((first, second)):
        cols = pl.ds(pl.multiple_of(col * LANES, LANES), LANES)
        to = pl.ds(LANES * half, LANES)
        for row, at, count in (
            (gy * ROWS, TILE, ROWS),
            (up_gy * ROWS + ROWS - TILE, 0, TILE),
            (down_gy * ROWS, TILE + ROWS, TILE),
        ):
            rows = pl.ds(pl.multiple_of(row, TILE), count)
            n = len(copies)
            copies.append(
                pltpu.make_async_copy(
                    height_hbm.at[:, rows, cols], height.at[:, pl.ds(at, count), to], field_sem.at[n]
                )
            )
            copies.append(
                pltpu.make_async_copy(
                    kind_hbm.at[rows, cols], kind.at[pl.ds(at, count), to], field_sem.at[n + 1]
                )
            )
    for copy in copies:
        copy.start()

    def pop_copy(g):
        rows = pl.ds(pl.multiple_of(TILE * g, TILE), TILE)
        return pltpu.make_async_copy(pop_hbm.at[:, rows, :], pop.at[:, rows, :], pop_sem.at[g])

    for g in range(GROUPS):
        pop_copy(g).start()

    wide = 4 * LANES
    cell = lax.broadcasted_iota(i32, (2 * LANES, wide), 0)
    place = lax.broadcasted_iota(i32, (2 * LANES, wide), 1)
    spread = (cell == offset + place // CZ).astype(f32)

    def widen(values):
        return jnp.dot(values.astype(f32), spread, preferred_element_type=f32)

    def active(row, col, j):
        return (owner_ref[j, row, col] >= 0).astype(f32)

    next_gx = lax.rem(gx + 1, NDEV)

    def act_tile(row, by, c):
        return active(row, gx, BXD * by + c) if c < BXD else active(row, next_gx, BXD * by)

    for copy in copies:
        copy.wait()
    kinds = widen(kind[...])
    value = wet_ref[0]
    for n in range(1, NCLS):
        value = jnp.where(kinds > n - 0.5, wet_ref[n], value)
    level = 1.0 + value
    lane = lane_of()
    depth = (lane % CZ).astype(f32)
    sub_low = row_of() < 4
    low, high = (TILE + ROWS, 0)
    for s in range(2):
        tall = widen(height[s])
        for c in range(4):
            cols = slice(LANES * c, LANES * (c + 1))
            for by in range(BYD):
                act = act_tile(gy, by, c)
                for rr in range(4):
                    g = 4 * by + rr
                    rows = slice(TILE * (g + 1), TILE * (g + 2))
                    fluid = depth < tall[rows, cols] * act
                    gas_ref[s, g, c] = jnp.where(fluid, 0.0, level[rows, cols])
            act = jnp.where(sub_low, act_tile(down_gy, 0, c), act_tile(up_gy, 1, c))
            here = jnp.where(sub_low, tall[low : low + TILE, cols], tall[high : high + TILE, cols])
            wall = jnp.where(sub_low, level[low : low + TILE, cols], level[high : high + TILE, cols])
            gas_ref[s, GROUPS, c] = jnp.where(depth < here * act, 0.0, wall)
    packed = gas_ref[0, 0, 3]
    for g in range(1, GROUPS):
        packed = jnp.where(lane >= 16 * g, pltpu.roll(gas_ref[0, g, 3], 16 * g, 1), packed)
    packed_ref[...] = packed

    def step(g, carry):
        pop_copy(g).wait()
        rows = pl.ds(pl.multiple_of(TILE * g, TILE), TILE)
        for c in range(3):
            f = [pop[i, rows, LANES * c : LANES * (c + 1)] for i in range(Q)]
            out = collide(f, gas_ref[0, g, c])
            for i in range(Q):
                post_ref[i, c, rows, :] = out[i]
        return carry

    lax.fori_loop(0, GROUPS, step, 0)
    for i in range(Q):
        up_ref[2 * i : 2 * i + 2, :] = pop[i, 0:2, :]
        down_ref[2 * i : 2 * i + 2, :] = pop[i, ROWS - 2 : ROWS, :]


def own_part(owner, wetting, populations, heights, wall_class):
    return pl.pallas_call(
        own_kernel,
        in_specs=[SMEM_SPEC, SMEM_SPEC, HBM_SPEC, HBM_SPEC, HBM_SPEC],
        out_specs=[VMEM_SPEC] * 5,
        out_shape=[
            OWN_SHAPE,
            jax.ShapeDtypeStruct((2, GROUPS + 1, 4, TILE, LANES), f32),
            jax.ShapeDtypeStruct((TILE, LANES), f32),
            jax.ShapeDtypeStruct((2 * Q + 2, 3 * LANES), f32),
            jax.ShapeDtypeStruct((2 * Q + 2, 3 * LANES), f32),
        ],
        scratch_shapes=[
            pltpu.VMEM((Q, ROWS, 3 * LANES), f32),
            pltpu.VMEM((2, ROWS + 2 * TILE, 2 * LANES), i32),
            pltpu.VMEM((ROWS + 2 * TILE, 2 * LANES), i32),
            pltpu.SemaphoreType.DMA((GROUPS,)),
            pltpu.SemaphoreType.DMA((12,)),
        ],
        compiler_params=params(50 * MIB),
        cost_estimate=pl.CostEstimate(flops=8_000_000, bytes_accessed=8_000_000, transcendentals=0),
        name="own_cells",
    )(owner, wetting, populations, heights, wall_class)


def pack_rows_kernel(up_in, down_in, right_ref, up_ref, down_ref):
    up_ref[:, 0 : 3 * LANES] = up_in[...]
    down_ref[:, 0 : 3 * LANES] = down_in[...]
    for i in range(Q):
        up_ref[2 * i : 2 * i + 2, 3 * LANES :] = right_ref[i, 0:2, :]
        last = pltpu.roll(right_ref[i], 16, 1)
        down_ref[2 * i : 2 * i + 2, 3 * LANES :] = last[TILE - 2 : TILE]


def pack_rows(up, down, right):
    return pl.pallas_call(
        pack_rows_kernel,
        in_specs=[VMEM_SPEC] * 3,
        out_specs=[VMEM_SPEC] * 2,
        out_shape=[EDGE_SHAPE, EDGE_SHAPE],
        compiler_params=params(),
        name="pack_rows",
    )(up, down, right)


def store_running(load, out_ref, halves_ref, by, rr, lane):
    for c in range(3):
        j = BXD * by + c
        tail = pull(load, TAIL, c, lane, 8)
        for n, i in enumerate(SENT):
            value = pull(load, i, c, lane, 8)
            if i in CARRIERS:
                back = 3 - CARRIERS.index(i)
                value = jnp.where(lane % CZ == CZ - 1, pltpu.roll(tail, back, 1), value)
            if n < NDEV:
                out_ref[n, B * j + TILE * rr : B * j + TILE * (rr + 1), :] = value
            else:
                m = 8 * (n - NDEV) + 2 * rr
                halves_ref[m, 4 * j : 4 * j + 4, :] = value[0:4]
                halves_ref[m + 1, 4 * j : 4 * j + 4, :] = value[4:8]


INNER = ((0, 2), (0, 3), (1, 0), (1, 1))
OUTER = ((0, 0), (0, 1), (1, 2), (1, 3))


def message_copy(buf, out_hbm, sem, j, start):
    rows = pl.ds(B * j + start, 2 * TILE)
    return pltpu.make_async_copy(buf.at[:, rows, :], out_hbm.at[:, rows, :], sem.at[j])


def inner_kernel(own_ref, gas_ref, packed_ref, right_ref, post_ref, two_ref, halves_ref, out_hbm, buf, sem):
    lane = lane_of()
    out = collide([right_ref[i] for i in range(Q)], packed_ref[...])
    for i in range(Q):
        for g in range(GROUPS):
            tile = out[i] if g == 0 else pltpu.roll(out[i], LANES - 16 * g, 1)
            post_ref[i, TILE * g : TILE * (g + 1), :] = tile

    def second(g, carry):
        def load(i, c, dy):
            rows = pl.ds(TILE * g - dy, TILE)
            return own_ref[i, c, rows, :] if c < 3 else post_ref[i, rows, :]

        for c in range(4):
            out = collide([pull(load, i, c, lane, 0) for i in range(Q)], gas_ref[1, g, c])
            for i in range(Q):
                two_ref[i, c, pl.ds(pl.multiple_of(TILE * g, TILE), TILE), :] = out[i]
        return carry

    lax.fori_loop(1, GROUPS - 1, second, 0)
    copies = []
    for by, rr in INNER:
        at = TILE * (4 * by + rr)
        store_running(
            lambda i, c, dy: two_ref[i, c, at - dy : at - dy + TILE, :], buf, halves_ref, by, rr, lane
        )
        if rr % 2 == 1:
            for c in range(3):
                copies.append(message_copy(buf, out_hbm, sem, BXD * by + c, TILE * (rr - 1)))
                copies[-1].start()
    for copy in copies:
        copy.wait()


def inner_part(own, gas, packed, right):
    return pl.pallas_call(
        inner_kernel,
        in_specs=[VMEM_SPEC] * 4,
        out_specs=[VMEM_SPEC, VMEM_SPEC, VMEM_SPEC, HBM_SPEC],
        out_shape=[RIGHT_SHAPE, TWO_SHAPE, HALVES_SHAPE, MESSAGE_SHAPE],
        scratch_shapes=[pltpu.VMEM((NDEV, BLK * B, LANES), f32), pltpu.SemaphoreType.DMA((BLK,))],
        compiler_params=params(),
        cost_estimate=pl.CostEstimate(flops=8_000_000, bytes_accessed=8_000_000, transcendentals=0),
        name="inner_rows",
    )(own, gas, packed, right)


def edge_kernel(
    message_in,
    halves_in,
    own_ref,
    post_ref,
    two_ref,
    gas_ref,
    below_ref,
    above_ref,
    out_hbm,
    halo,
    top,
    bottom,
    top_two,
    bottom_two,
    buf,
    halves,
    sem,
    half_sem,
):
    lane = lane_of()
    sub_low = row_of() < 4
    tall = ROWS - TILE

    halves[...] = halves_in[...]
    halo[...] = jnp.ones(halo.shape, f32)
    for i in range(Q):
        for c in range(4):
            cols = slice(LANES * c, LANES * (c + 1))
            halo[i, c, 0:2, :] = below_ref[2 * i : 2 * i + 2, cols]
            halo[i, c, TILE - 2 : TILE, :] = above_ref[2 * i : 2 * i + 2, cols]
            first = own_ref[i, c, 0:TILE, :] if c < 3 else post_ref[i, 0:TILE, :]
            last = own_ref[i, c, tall:ROWS, :] if c < 3 else post_ref[i, tall:ROWS, :]
            top[i, c, 16:24, :] = first
            bottom[i, c, 8:16, :] = last
            top_two[i, c, 24:32, :] = two_ref[i, c, TILE : 2 * TILE, :]
            bottom_two[i, c, 8:16, :] = two_ref[i, c, tall - TILE : tall, :]
    for c in range(4):
        out = collide([halo[i, c] for i in range(Q)], gas_ref[0, GROUPS, c])
        for i in range(Q):
            top[i, c, 8:16, :] = out[i]
            bottom[i, c, 16:24, :] = out[i]

    def load_first(i, c, dy):
        if dy == 1:
            return top[i, c, 15:23, :]
        return own_ref[i, c, -dy : TILE - dy, :] if c < 3 else post_ref[i, -dy : TILE - dy, :]

    def load_last(i, c, dy):
        if dy == -1:
            return bottom[i, c, 9:17, :]
        return own_ref[i, c, tall - dy : ROWS - dy, :] if c < 3 else post_ref[i, tall - dy : ROWS - dy, :]

    def load_halo(i, c, dy):
        return jnp.where(sub_low, bottom[i, c, 16 - dy : 24 - dy, :], top[i, c, 8 - dy : 16 - dy, :])

    for c in range(4):
        out = collide([pull(load_first, i, c, lane, 0) for i in range(Q)], gas_ref[1, 0, c])
        for i in range(Q):
            top_two[i, c, 16:24, :] = out[i]
        out = collide([pull(load_last, i, c, lane, 0) for i in range(Q)], gas_ref[1, GROUPS - 1, c])
        for i in range(Q):
            bottom_two[i, c, 16:24, :] = out[i]
        out = collide([pull(load_halo, i, c, lane, 0) for i in range(Q)], gas_ref[1, GROUPS, c])
        for i in range(Q):
            top_two[i, c, 8:16, :] = out[i]
            bottom_two[i, c, 24:32, :] = out[i]

    copies = []
    for by, rr in OUTER:
        g = 4 * by + rr

        def load(i, c, dy):
            if by == 0 and (g == 0 or dy == 1):
                return top_two[i, c, 16 + TILE * g - dy : 24 + TILE * g - dy, :]
            if by == 1 and (g == GROUPS - 1 or dy == -1):
                at = TILE * (g - GROUPS + 3) - dy
                return bottom_two[i, c, at : at + TILE, :]
            return two_ref[i, c, TILE * g - dy : TILE * (g + 1) - dy, :]

        store_running(load, buf, halves, by, rr, lane)
        if rr % 2 == 1:
            for c in range(3):
                copies.append(message_copy(buf, out_hbm, sem, BXD * by + c, TILE * (rr - 1)))
                copies[-1].start()
    copies.append(
        pltpu.make_async_copy(halves, out_hbm.at[:, pl.ds(BLK * B, 4 * BLK), :], half_sem)
    )
    copies[-1].start()
    for copy in copies:
        copy.wait()


def edge_part(message, halves, own, post, two, gas, below, above):
    return pl.pallas_call(
        edge_kernel,
        in_specs=[HBM_SPEC] + [VMEM_SPEC] * 7,
        out_specs=HBM_SPEC,
        out_shape=MESSAGE_SHAPE,
        input_output_aliases={0: 0},
        scratch_shapes=[
            pltpu.VMEM((Q, 4, TILE, LANES), f32),
            pltpu.VMEM((Q, 4, 3 * TILE, LANES), f32),
            pltpu.VMEM((Q, 4, 4 * TILE, LANES), f32),
            pltpu.VMEM((Q, 4, 4 * TILE, LANES), f32),
            pltpu.VMEM((Q, 4, 4 * TILE, LANES), f32),
            pltpu.VMEM((NDEV, BLK * B, LANES), f32),
            pltpu.VMEM((NDEV, 4 * BLK, LANES), f32),
            pltpu.SemaphoreType.DMA((BLK,)),
            pltpu.SemaphoreType.DMA,
        ],
        compiler_params=params(),
        cost_estimate=pl.CostEstimate(flops=8_000_000, bytes_accessed=8_000_000, transcendentals=0),
        name="edge_rows",
    )(message, halves, own, post, two, gas, below, above)


def sort_kernel(table_ref, in_ref, out_ref):
    lane = lane_of()
    sub_low = row_of() < 4
    count = NDEV * CAP

    def receiver(d, carry):
        halves = []
        for k in range(CAP):
            n = d * CAP + k
            valid = table_ref[n] >= 0
            s, j = (table_ref[count + n], table_ref[2 * count + n])
            ps, pj = (table_ref[3 * count + n], table_ref[4 * count + n])
            for t in range(4):
                now = in_ref[s, pl.ds(pl.multiple_of(B * j + TILE * t, TILE), TILE), :]
                before = in_ref[ps, pl.ds(pl.multiple_of(B * pj + TILE * t, TILE), TILE), :]
                tile = pltpu.roll(jnp.where(lane >= 120, before, now), 8, 1)
                out_ref[d, B * k + TILE * t : B * k + TILE * (t + 1), :] = jnp.where(valid, tile, 0.0)

            def half(s, j):
                pair = lax.shift_right_logical(j, 1)
                tile = in_ref[s, pl.ds(pl.multiple_of(BLK * B + TILE * pair, TILE), TILE), :]
                return jnp.where(j - 2 * pair == k % 2, tile, pltpu.roll(tile, 4, 0))

            tile = pltpu.roll(jnp.where(lane >= 120, half(ps, pj), half(s, j)), 8, 1)
            halves.append(jnp.where(valid, tile, 0.0))
        for pair in range(CAP // 2):
            at = CAP * B + TILE * pair
            out_ref[d, at : at + TILE, :] = jnp.where(sub_low, halves[2 * pair], halves[2 * pair + 1])
        return carry

    lax.fori_loop(0, NDEV, receiver, 0, unroll=4)


def sort_blocks(table, arrived):
    return pl.pallas_call(
        sort_kernel,
        in_specs=[SMEM_SPEC, VMEM_SPEC],
        out_specs=VMEM_SPEC,
        out_shape=jax.ShapeDtypeStruct((NDEV, SLOTS, LANES), f32),
        compiler_params=params(),
        name="sort_blocks",
    )(table, arrived)


def restore_kernel(taken_ref, in_ref, out_hbm, buf, sem):
    lane = lane_of()
    sub_low = row_of() < 4
    top = lane % CZ == CZ - 1
    place = lane % CZ

    def slot(k, taken, t):
        rows = slice(B * k + TILE * t, B * k + TILE * (t + 1))
        planes = {m: in_ref[m, rows, :] for m in range(NDEV)}
        pair = CAP * B + TILE * (k // 2)
        for p in range(2):
            a = in_ref[8 * p + 2 * t, pair : pair + TILE, :]
            b = in_ref[8 * p + 2 * t + 1, pair : pair + TILE, :]
            if k % 2 == 0:
                b = pltpu.roll(b, 4, 0)
            else:
                a = pltpu.roll(a, 4, 0)
            planes[NDEV + p] = jnp.where(sub_low, a, b)
        at = slice(TILE * t, TILE * (t + 1))
        last = taken * jnp.float32(WEIGHTS[TAIL])
        parts = [pltpu.roll(planes[i], LANES - 3 + n, 1) for n, i in enumerate(CARRIERS)]
        tail = jnp.where(place == 0, parts[0], jnp.where(place == 1, parts[1], parts[2]))
        buf[k, TAIL, at, :] = jnp.where(top, last, tail)
        for n, i in enumerate(SENT):
            value = planes[n]
            if i in FIXED_TOP:
                value = jnp.where(top, taken * jnp.float32(WEIGHTS[i]), value)
            buf[k, i, at, :] = value

    copies = [pltpu.make_async_copy(buf.at[k], out_hbm.at[0, k], sem.at[k]) for k in range(CAP)]
    for k in range(CAP):
        taken = (taken_ref[0] > k).astype(f32)
        for t in range(4):
            slot(k, taken, t)
        copies[k].start()
    for copy in copies:
        copy.wait()


def restore(taken, arrived):
    return pl.pallas_call(
        restore_kernel,
        in_specs=[SMEM_SPEC, VMEM_SPEC],
        out_specs=HBM_SPEC,
        out_shape=jax.ShapeDtypeStruct((1, CAP, Q, B, LANES), f32),
        scratch_shapes=[pltpu.VMEM((CAP, Q, B, LANES), f32), pltpu.SemaphoreType.DMA((CAP,))],
        compiler_params=params(),
        name="restore",
    )(taken, arrived)


def tables(owner, gy, gx):
    flat = lax.dynamic_index_in_dim(owner, gy, 0, keepdims=False).reshape(-1)
    number = jnp.arange(NDEV * BLK)
    same = (flat[:, None] == flat[None, :]) & (number[None, :] < number[:, None])
    slot = jnp.sum(same.astype(i32), axis=1)
    target = jnp.where(flat >= 0, flat * CAP + slot, -1)
    hit = target[:, None] == jnp.arange(NDEV * CAP)[None, :]
    table = jnp.max(jnp.where(hit, number[:, None], -1), axis=0).astype(i32)
    block = jnp.maximum(table, 0)
    s, j = (block // BLK, block % BLK)
    at_edge = j % BXD == 0
    before_s = jnp.where(at_edge, (s + NDEV - 1) % NDEV, s)
    before_j = jnp.where(at_edge, j + BXD - 1, j - 1)
    taken = jnp.sum((flat == gx).astype(i32)).reshape(1)
    return (jnp.concatenate([table, s, j, before_s, before_j]), taken)


def local(populations, heights, wall_class, wetting, owner):
    gy = lax.axis_index("gy")
    gx = lax.axis_index("gx")
    n_gy = lax.axis_size("gy")
    right = lax.ppermute(pack_cols(populations), "gx", [(i, (i - 1) % NDEV) for i in range(NDEV)])
    own, gas, packed, up, down = own_part(
        owner.transpose(2, 0, 1), wetting, populations, heights, wall_class
    )
    up, down = pack_rows(up, down, right)
    below = lax.ppermute(up, "gy", [(i, (i - 1) % n_gy) for i in range(n_gy)])
    above = lax.ppermute(down, "gy", [(i, (i + 1) % n_gy) for i in range(n_gy)])
    post, two, halves, message = inner_part(own, gas, packed, right)
    message = edge_part(message, halves, own, post, two, gas, below, above)
    table, taken = tables(owner, gy, gx)
    gathered = lax.all_to_all(message, "gx", split_axis=0, concat_axis=0, tiled=True)
    chosen = sort_blocks(table, gathered)
    arrived = lax.all_to_all(chosen, "gx", split_axis=0, concat_axis=0, tiled=True)
    return restore(taken, arrived)


def solution(mesh):
    return jax.shard_map(
        local,
        mesh=mesh,
        in_specs=(P(None, "gy", "gx"), P(), P(), P(), P()),
        out_specs=P("gy", "gx", None, None, None),
        check_vma=False,
    )
```

```python
import functools

import jax
import jax.numpy as jnp
import numpy as np
from jax import lax
from jax.experimental import pallas as pl
from jax.experimental.pallas import tpu as pltpu
from jax.sharding import PartitionSpec as P

B = 32
CZ = 4
BXD = 3
BYD = 2
CAP = 4
NCLS = 4
BLK = BXD * BYD
Q = 19
TILE = 8
LANES = 128
ROWS = 64
GROUPS = ROWS // TILE
SENT = [i for i in range(Q) if i != 17]
TAIL = 17
NDEV = 16
PIECE = BLK * (B + 4)
SLOTS = CAP * (B + 4)

VELOCITY = [
    (0, 0, 0),
    (1, 0, 0),
    (-1, 0, 0),
    (0, 1, 0),
    (0, -1, 0),
    (0, 0, 1),
    (0, 0, -1),
    (1, 1, 0),
    (-1, -1, 0),
    (1, -1, 0),
    (-1, 1, 0),
    (1, 0, 1),
    (-1, 0, -1),
    (1, 0, -1),
    (-1, 0, 1),
    (0, 1, 1),
    (0, -1, -1),
    (0, 1, -1),
    (0, -1, 1),
]
WEIGHTS = [1.0 / 3.0] + [1.0 / 18.0] * 6 + [1.0 / 36.0] * 12
OPPOSITE = [0, 2, 1, 4, 3, 6, 5, 8, 7, 10, 9, 12, 11, 14, 13, 16, 15, 18, 17]
CARRIERS = (6, 12, 13)
FIXED_TOP = (6, 12, 13, 16)

f32 = jnp.float32
i32 = jnp.int32
MIB = 1024 * 1024
PACK_LIMIT = 52 * MIB
OWN_LIMIT = 50 * MIB


def params(limit=16 * MIB):
    return pltpu.CompilerParams(vmem_limit_bytes=limit)


VMEM_SPEC = pl.BlockSpec(memory_space=pltpu.VMEM)
HBM_SPEC = pl.BlockSpec(memory_space=pltpu.HBM)
SMEM_SPEC = pl.BlockSpec(memory_space=pltpu.SMEM)
OWN_SHAPE = jax.ShapeDtypeStruct((Q, 3, ROWS, LANES), f32)
TWO_SHAPE = jax.ShapeDtypeStruct((Q, 4, ROWS, LANES), f32)
LEFT_SHAPE = jax.ShapeDtypeStruct((Q, ROWS, LANES), f32)
EDGE_SHAPE = jax.ShapeDtypeStruct((2 * Q + 2, 4 * LANES), f32)
MESSAGE_SHAPE = jax.ShapeDtypeStruct((NDEV, PIECE, LANES), f32)
HALVES_SHAPE = jax.ShapeDtypeStruct((NDEV, 4 * BLK, LANES), f32)


def lane_of():
    return lax.broadcasted_iota(i32, (TILE, LANES), 1)


def row_of():
    return lax.broadcasted_iota(i32, (TILE, LANES), 0)


def collide(f, gas):
    pairs = [(i, i + 1) for i in range(1, Q, 2)]
    total = {i: f[i] + f[o] for i, o in pairs}
    diff = {i: f[i] - f[o] for i, o in pairs}
    rho = f[0]
    for i, _ in pairs:
        rho = rho + total[i]
    jx = diff[1] + diff[7] + diff[9] + diff[11] + diff[13]
    jy = diff[3] + diff[7] - diff[9] + diff[15] + diff[17]
    jz = diff[5] + diff[11] - diff[13] + diff[15] - diff[17]
    inv = 1.0 / rho
    scaled = rho - 1.5 * inv * (jx * jx + jy * jy + jz * jz)
    along = {
        1: jx,
        3: jy,
        5: jz,
        7: jx + jy,
        9: jx - jy,
        11: jx + jz,
        13: jx - jz,
        15: jy + jz,
        17: jy - jz,
    }
    is_gas = gas > 0
    out = [None] * Q
    out[0] = jnp.where(
        is_gas, WEIGHTS[0] * gas, -0.6 * f[0] + (1.6 * WEIGHTS[0]) * scaled
    )
    for first, last in ((1, 5), (7, 17)):
        w = WEIGHTS[first]
        base = (1.6 * w) * scaled
        bend = (7.2 * w) * inv
        held = w * gas
        for i in range(first, last + 1, 2):
            cj = along[i]
            even = base + bend * (cj * cj) - 0.3 * total[i]
            odd = 0.25 * diff[i] + (1.5 * w) * cj
            out[i] = jnp.where(is_gas, held, even + odd)
            out[i + 1] = jnp.where(is_gas, held, even - odd)
    return out


def shifted(load, c, shift, lane):
    if shift == 0:
        return load(c)
    here = load(c)
    if shift > 0:
        if c != 3:
            here = jnp.where(lane >= LANES - shift, load((c + 3) % 4), here)
        return pltpu.roll(here, shift, 1)
    if c != 2:
        here = jnp.where(lane < -shift, load((c + 1) % 4), here)
    return pltpu.roll(here, LANES + shift, 1)


def pull(load, i, c, lane, extra):
    cx, cy, cz = VELOCITY[i]
    moved = shifted(lambda t: load(i, t, cy), c, 4 * cx + cz + extra, lane)
    if cz == 1:
        wall = shifted(lambda t: load(OPPOSITE[i], t, 0), c, extra, lane)
        moved = jnp.where(lane % CZ == 0, wall, moved)
    elif cz == -1:
        moved = jnp.where(lane % CZ == CZ - 1, jnp.float32(WEIGHTS[i]), moved)
    return moved


def pack_cols_kernel(pop_hbm, out_ref, buf, sem):
    copies = []
    for g in range(GROUPS):
        rows = pl.ds(TILE * g, TILE)
        copies.append(
            pltpu.make_async_copy(
                pop_hbm.at[:, rows, pl.ds(2 * LANES, LANES)], buf.at[:, rows, :], sem.at[g]
            )
        )
        copies[-1].start()
    lane = lane_of()
    for copy in copies:
        copy.wait()
    for i in range(Q):
        packed = pltpu.roll(buf[i, 0:TILE, :], 16, 1)
        for g in range(1, GROUPS):
            last = buf[i, TILE * g : TILE * (g + 1), :]
            if g < GROUPS - 1:
                last = pltpu.roll(last, 16 * (g + 1), 1)
            packed = jnp.where(lane >= 16 * g, last, packed)
        out_ref[i] = packed


def pack_cols(populations):
    return pl.pallas_call(
        pack_cols_kernel,
        in_specs=[HBM_SPEC],
        out_specs=VMEM_SPEC,
        out_shape=jax.ShapeDtypeStruct((Q, TILE, LANES), f32),
        scratch_shapes=[pltpu.VMEM((Q, ROWS, LANES), f32), pltpu.SemaphoreType.DMA((GROUPS,))],
        compiler_params=params(PACK_LIMIT),
        name="pack_cols",
    )(populations)


def own_kernel(
    owner_ref,
    wet_ref,
    pop_hbm,
    height_hbm,
    kind_hbm,
    post_ref,
    gas_ref,
    packed_ref,
    up_ref,
    down_ref,
    pop,
    height,
    kind,
    pop_sem,
    field_sem,
):
    gy, gx = (lax.axis_index("gy"), lax.axis_index("gx"))
    n_gy = height_hbm.shape[1] // ROWS
    n_x = height_hbm.shape[2] // LANES
    start = lax.rem(gx * (BXD * B) + n_x * LANES - 4, n_x * LANES)
    first = start // LANES
    offset = start - first * LANES
    second = lax.rem(first + 1, n_x)
    up_gy, down_gy = (lax.rem(gy + n_gy - 1, n_gy), lax.rem(gy + 1, n_gy))
    copies = []
    for half, col in enumerate((first, second)):
        cols = pl.ds(pl.multiple_of(col * LANES, LANES), LANES)
        to = pl.ds(LANES * half, LANES)
        for row, at, count in (
            (gy * ROWS, TILE, ROWS),
            (up_gy * ROWS + ROWS - TILE, 0, TILE),
            (down_gy * ROWS, TILE + ROWS, TILE),
        ):
            rows = pl.ds(pl.multiple_of(row, TILE), count)
            n = len(copies)
            copies.append(
                pltpu.make_async_copy(
                    height_hbm.at[:, rows, cols], height.at[:, pl.ds(at, count), to], field_sem.at[n]
                )
            )
            copies.append(
                pltpu.make_async_copy(
                    kind_hbm.at[rows, cols], kind.at[pl.ds(at, count), to], field_sem.at[n + 1]
                )
            )
    for copy in copies:
        copy.start()

    def pop_copy(g):
        rows = pl.ds(pl.multiple_of(TILE * g, TILE), TILE)
        return pltpu.make_async_copy(pop_hbm.at[:, rows, :], pop.at[:, rows, :], pop_sem.at[g])

    for g in range(GROUPS):
        pop_copy(g).start()

    wide = 4 * LANES
    cell = lax.broadcasted_iota(i32, (2 * LANES, wide), 0)
    place = lax.broadcasted_iota(i32, (2 * LANES, wide), 1)
    spread = (cell == offset + 4 + place // CZ - jnp.where(place >= 3 * LANES, LANES, 0)).astype(f32)

    def widen(values):
        return jnp.dot(values.astype(f32), spread, preferred_element_type=f32)

    def active(row, col, j):
        return (owner_ref[j, row, col] >= 0).astype(f32)

    left_gx = lax.rem(gx + NDEV - 1, NDEV)

    def act_tile(row, by, c):
        return active(row, gx, BXD * by + c) if c < 3 else active(row, left_gx, BXD * by + 2)

    for copy in copies:
        copy.wait()
    kinds = widen(kind[...])
    value = wet_ref[0]
    for n in range(1, NCLS):
        value = jnp.where(kinds > n - 0.5, wet_ref[n], value)
    level = 1.0 + value
    lane = lane_of()
    depth = (lane % CZ).astype(f32)
    sub_low = row_of() < 4
    low, high = (TILE + ROWS, 0)
    for s in range(2):
        tall = widen(height[s])
        for c in range(4):
            cols = slice(LANES * c, LANES * (c + 1))
            for by in range(BYD):
                act = act_tile(gy, by, c)
                for rr in range(4):
                    g = 4 * by + rr
                    rows = slice(TILE * (g + 1), TILE * (g + 2))
                    fluid = depth < tall[rows, cols] * act
                    gas_ref[s, g, c] = jnp.where(fluid, 0.0, level[rows, cols])
            act = jnp.where(sub_low, act_tile(down_gy, 0, c), act_tile(up_gy, 1, c))
            here = jnp.where(sub_low, tall[low : low + TILE, cols], tall[high : high + TILE, cols])
            wall = jnp.where(sub_low, level[low : low + TILE, cols], level[high : high + TILE, cols])
            gas_ref[s, GROUPS, c] = jnp.where(depth < here * act, 0.0, wall)
    packed = pltpu.roll(gas_ref[0, 0, 3], 16, 1)
    for g in range(1, GROUPS):
        tile = gas_ref[0, g, 3]
        if g < GROUPS - 1:
            tile = pltpu.roll(tile, 16 * (g + 1), 1)
        packed = jnp.where(lane >= 16 * g, tile, packed)
    packed_ref[...] = packed

    def step(g, carry):
        pop_copy(g).wait()
        rows = pl.ds(pl.multiple_of(TILE * g, TILE), TILE)
        for c in range(3):
            f = [pop[i, rows, LANES * c : LANES * (c + 1)] for i in range(Q)]
            out = collide(f, gas_ref[0, g, c])
            for i in range(Q):
                post_ref[i, c, rows, :] = out[i]
        return carry

    lax.fori_loop(0, GROUPS, step, 0)
    for i in range(Q):
        up_ref[2 * i : 2 * i + 2, :] = pop[i, 0:2, :]
        down_ref[2 * i : 2 * i + 2, :] = pop[i, ROWS - 2 : ROWS, :]


def own_part(owner, wetting, populations, heights, wall_class):
    return pl.pallas_call(
        own_kernel,
        in_specs=[SMEM_SPEC, SMEM_SPEC, HBM_SPEC, HBM_SPEC, HBM_SPEC],
        out_specs=[VMEM_SPEC] * 5,
        out_shape=[
            OWN_SHAPE,
            jax.ShapeDtypeStruct((2, GROUPS + 1, 4, TILE, LANES), f32),
            jax.ShapeDtypeStruct((TILE, LANES), f32),
            jax.ShapeDtypeStruct((2 * Q + 2, 3 * LANES), f32),
            jax.ShapeDtypeStruct((2 * Q + 2, 3 * LANES), f32),
        ],
        scratch_shapes=[
            pltpu.VMEM((Q, ROWS, 3 * LANES), f32),
            pltpu.VMEM((2, ROWS + 2 * TILE, 2 * LANES), i32),
            pltpu.VMEM((ROWS + 2 * TILE, 2 * LANES), i32),
            pltpu.SemaphoreType.DMA((GROUPS,)),
            pltpu.SemaphoreType.DMA((12,)),
        ],
        compiler_params=params(OWN_LIMIT),
        cost_estimate=pl.CostEstimate(flops=8_000_000, bytes_accessed=8_000_000, transcendentals=0),
        name="own_cells",
    )(owner, wetting, populations, heights, wall_class)


def pack_rows_kernel(up_in, down_in, left_ref, up_ref, down_ref):
    up_ref[:, 0 : 3 * LANES] = up_in[...]
    down_ref[:, 0 : 3 * LANES] = down_in[...]
    for i in range(Q):
        first = pltpu.roll(left_ref[i], LANES - 16, 1)
        up_ref[2 * i : 2 * i + 2, 3 * LANES :] = first[0:2]
        down_ref[2 * i : 2 * i + 2, 3 * LANES :] = left_ref[i, TILE - 2 : TILE, :]


def pack_rows(up, down, left):
    return pl.pallas_call(
        pack_rows_kernel,
        in_specs=[VMEM_SPEC] * 3,
        out_specs=[VMEM_SPEC] * 2,
        out_shape=[EDGE_SHAPE, EDGE_SHAPE],
        compiler_params=params(),
        name="pack_rows",
    )(up, down, left)


def store_running(load, out_ref, halves_ref, by, rr, lane):
    for c in range(3):
        j = BXD * by + c
        tail = pull(load, TAIL, c, lane, 8)
        for n, i in enumerate(SENT):
            value = pull(load, i, c, lane, 8)
            if i in CARRIERS:
                back = 3 - CARRIERS.index(i)
                value = jnp.where(lane % CZ == CZ - 1, pltpu.roll(tail, back, 1), value)
            if n < NDEV:
                out_ref[n, B * j + TILE * rr : B * j + TILE * (rr + 1), :] = value
            else:
                m = 8 * (n - NDEV) + 2 * rr
                halves_ref[m, 4 * j : 4 * j + 4, :] = value[0:4]
                halves_ref[m + 1, 4 * j : 4 * j + 4, :] = value[4:8]


INNER = ((0, 2), (0, 3), (1, 0), (1, 1))
OUTER = ((0, 0), (0, 1), (1, 2), (1, 3))


def message_copy(buf, out_hbm, sem, j, start):
    rows = pl.ds(B * j + start, 2 * TILE)
    return pltpu.make_async_copy(buf.at[:, rows, :], out_hbm.at[:, rows, :], sem.at[j])


def inner_kernel(own_ref, gas_ref, packed_ref, left_ref, post_ref, two_ref, halves_ref, out_hbm, buf, sem):
    lane = lane_of()
    out = collide([left_ref[i] for i in range(Q)], packed_ref[...])
    for i in range(Q):
        for g in range(GROUPS):
            tile = out[i] if g == GROUPS - 1 else pltpu.roll(out[i], LANES - 16 * (g + 1), 1)
            post_ref[i, TILE * g : TILE * (g + 1), :] = tile

    def second(g, carry):
        def load(i, c, dy):
            rows = pl.ds(TILE * g - dy, TILE)
            return own_ref[i, c, rows, :] if c < 3 else post_ref[i, rows, :]

        for c in range(4):
            out = collide([pull(load, i, c, lane, 0) for i in range(Q)], gas_ref[1, g, c])
            for i in range(Q):
                two_ref[i, c, pl.ds(pl.multiple_of(TILE * g, TILE), TILE), :] = out[i]
        return carry

    lax.fori_loop(1, GROUPS - 1, second, 0)
    copies = []
    for by, rr in INNER:
        at = TILE * (4 * by + rr)
        store_running(
            lambda i, c, dy: two_ref[i, c, at - dy : at - dy + TILE, :], buf, halves_ref, by, rr, lane
        )
        if rr % 2 == 1:
            for c in range(3):
                copies.append(message_copy(buf, out_hbm, sem, BXD * by + c, TILE * (rr - 1)))
                copies[-1].start()
    for copy in copies:
        copy.wait()


def inner_part(own, gas, packed, left):
    return pl.pallas_call(
        inner_kernel,
        in_specs=[VMEM_SPEC] * 4,
        out_specs=[VMEM_SPEC, VMEM_SPEC, VMEM_SPEC, HBM_SPEC],
        out_shape=[LEFT_SHAPE, TWO_SHAPE, HALVES_SHAPE, MESSAGE_SHAPE],
        scratch_shapes=[pltpu.VMEM((NDEV, BLK * B, LANES), f32), pltpu.SemaphoreType.DMA((BLK,))],
        compiler_params=params(),
        cost_estimate=pl.CostEstimate(flops=8_000_000, bytes_accessed=8_000_000, transcendentals=0),
        name="inner_rows",
    )(own, gas, packed, left)


def edge_kernel(
    table_ref,
    message_in,
    halves_in,
    own_ref,
    post_ref,
    two_ref,
    gas_ref,
    below_ref,
    above_ref,
    out_hbm,
    halo,
    top,
    bottom,
    top_two,
    bottom_two,
    buf,
    halves,
    sem,
    half_sem,
):
    lane = lane_of()
    sub_low = row_of() < 4
    tall = ROWS - TILE

    halves[...] = halves_in[...]
    halo[...] = jnp.ones(halo.shape, f32)
    for i in range(Q):
        for c in range(4):
            cols = slice(LANES * c, LANES * (c + 1))
            halo[i, c, 0:2, :] = below_ref[2 * i : 2 * i + 2, cols]
            halo[i, c, TILE - 2 : TILE, :] = above_ref[2 * i : 2 * i + 2, cols]
            first = own_ref[i, c, 0:TILE, :] if c < 3 else post_ref[i, 0:TILE, :]
            last = own_ref[i, c, tall:ROWS, :] if c < 3 else post_ref[i, tall:ROWS, :]
            top[i, c, 16:24, :] = first
            bottom[i, c, 8:16, :] = last
            top_two[i, c, 24:32, :] = two_ref[i, c, TILE : 2 * TILE, :]
            bottom_two[i, c, 8:16, :] = two_ref[i, c, tall - TILE : tall, :]
    for c in range(4):
        out = collide([halo[i, c] for i in range(Q)], gas_ref[0, GROUPS, c])
        for i in range(Q):
            top[i, c, 8:16, :] = out[i]
            bottom[i, c, 16:24, :] = out[i]

    def load_first(i, c, dy):
        if dy == 1:
            return top[i, c, 15:23, :]
        return own_ref[i, c, -dy : TILE - dy, :] if c < 3 else post_ref[i, -dy : TILE - dy, :]

    def load_last(i, c, dy):
        if dy == -1:
            return bottom[i, c, 9:17, :]
        return own_ref[i, c, tall - dy : ROWS - dy, :] if c < 3 else post_ref[i, tall - dy : ROWS - dy, :]

    def load_halo(i, c, dy):
        return jnp.where(sub_low, bottom[i, c, 16 - dy : 24 - dy, :], top[i, c, 8 - dy : 16 - dy, :])

    for c in range(4):
        out = collide([pull(load_first, i, c, lane, 0) for i in range(Q)], gas_ref[1, 0, c])
        for i in range(Q):
            top_two[i, c, 16:24, :] = out[i]
        out = collide([pull(load_last, i, c, lane, 0) for i in range(Q)], gas_ref[1, GROUPS - 1, c])
        for i in range(Q):
            bottom_two[i, c, 16:24, :] = out[i]
        out = collide([pull(load_halo, i, c, lane, 0) for i in range(Q)], gas_ref[1, GROUPS, c])
        for i in range(Q):
            top_two[i, c, 8:16, :] = out[i]
            bottom_two[i, c, 24:32, :] = out[i]

    copies = []
    for by, rr in OUTER:
        g = 4 * by + rr

        def load(i, c, dy):
            if by == 0 and (g == 0 or dy == 1):
                return top_two[i, c, 16 + TILE * g - dy : 24 + TILE * g - dy, :]
            if by == 1 and (g == GROUPS - 1 or dy == -1):
                at = TILE * (g - GROUPS + 3) - dy
                return bottom_two[i, c, at : at + TILE, :]
            return two_ref[i, c, TILE * g - dy : TILE * (g + 1) - dy, :]

        store_running(load, buf, halves, by, rr, lane)
        if rr % 2 == 1:
            for c in range(3):
                copies.append(message_copy(buf, out_hbm, sem, BXD * by + c, TILE * (rr - 1)))
                copies[-1].start()
    copies.append(
        pltpu.make_async_copy(halves, out_hbm.at[:, pl.ds(BLK * B, 4 * BLK), :], half_sem)
    )
    copies[-1].start()
    for copy in copies:
        copy.wait()


def edge_part(table, message, halves, own, post, two, gas, below, above):
    return pl.pallas_call(
        edge_kernel,
        in_specs=[SMEM_SPEC, HBM_SPEC] + [VMEM_SPEC] * 7,
        out_specs=HBM_SPEC,
        out_shape=MESSAGE_SHAPE,
        input_output_aliases={1: 0},
        scratch_shapes=[
            pltpu.VMEM((Q, 4, TILE, LANES), f32),
            pltpu.VMEM((Q, 4, 3 * TILE, LANES), f32),
            pltpu.VMEM((Q, 4, 4 * TILE, LANES), f32),
            pltpu.VMEM((Q, 4, 4 * TILE, LANES), f32),
            pltpu.VMEM((Q, 4, 4 * TILE, LANES), f32),
            pltpu.VMEM((NDEV, BLK * B, LANES), f32),
            pltpu.VMEM((NDEV, 4 * BLK, LANES), f32),
            pltpu.SemaphoreType.DMA((BLK,)),
            pltpu.SemaphoreType.DMA,
        ],
        compiler_params=params(),
        cost_estimate=pl.CostEstimate(flops=8_000_000, bytes_accessed=8_000_000, transcendentals=0),
        name="edge_rows",
    )(table, message, halves, own, post, two, gas, below, above)


def sort_kernel(table_ref, in_ref, out_ref):
    lane = lane_of()
    sub_low = row_of() < 4

    def receiver(d, carry):
        halves = []
        for k in range(CAP):
            n = d * CAP + k
            code = table_ref[n]
            valid = code >= 0
            code = jnp.maximum(code, 0)
            s, j = (code & 15, (code >> 4) & 7)
            ns, nj = ((code >> 8) & 15, code >> 12)
            for t in range(4):
                now = in_ref[s, pl.ds(pl.multiple_of(B * j + TILE * t, TILE), TILE), :]
                after = in_ref[ns, pl.ds(pl.multiple_of(B * nj + TILE * t, TILE), TILE), :]
                tile = pltpu.roll(jnp.where(lane < 8, after, now), LANES - 8, 1)
                out_ref[d, B * k + TILE * t : B * k + TILE * (t + 1), :] = jnp.where(valid, tile, 0.0)

            def half(s, j):
                pair = lax.shift_right_logical(j, 1)
                tile = in_ref[s, pl.ds(pl.multiple_of(BLK * B + TILE * pair, TILE), TILE), :]
                return jnp.where(j - 2 * pair == k % 2, tile, pltpu.roll(tile, 4, 0))

            tile = pltpu.roll(jnp.where(lane < 8, half(ns, nj), half(s, j)), LANES - 8, 1)
            halves.append(jnp.where(valid, tile, 0.0))
        for pair in range(CAP // 2):
            at = CAP * B + TILE * pair
            out_ref[d, at : at + TILE, :] = jnp.where(sub_low, halves[2 * pair], halves[2 * pair + 1])
        return carry

    lax.fori_loop(0, NDEV, receiver, 0, unroll=4)


def sort_blocks(table, arrived):
    return pl.pallas_call(
        sort_kernel,
        in_specs=[SMEM_SPEC, VMEM_SPEC],
        out_specs=VMEM_SPEC,
        out_shape=jax.ShapeDtypeStruct((NDEV, SLOTS, LANES), f32),
        compiler_params=params(),
        name="sort_blocks",
    )(table, arrived)


def restore_kernel(table_ref, in_ref, out_hbm, buf, sem):
    lane = lane_of()
    sub_low = row_of() < 4
    top = lane % CZ == CZ - 1
    place = lane % CZ

    def slot(k, taken, t):
        rows = slice(B * k + TILE * t, B * k + TILE * (t + 1))
        planes = {m: in_ref[m, rows, :] for m in range(NDEV)}
        pair = CAP * B + TILE * (k // 2)
        for p in range(2):
            a = in_ref[8 * p + 2 * t, pair : pair + TILE, :]
            b = in_ref[8 * p + 2 * t + 1, pair : pair + TILE, :]
            if k % 2 == 0:
                b = pltpu.roll(b, 4, 0)
            else:
                a = pltpu.roll(a, 4, 0)
            planes[NDEV + p] = jnp.where(sub_low, a, b)
        at = slice(TILE * t, TILE * (t + 1))
        last = taken * jnp.float32(WEIGHTS[TAIL])
        parts = [pltpu.roll(planes[i], LANES - 3 + n, 1) for n, i in enumerate(CARRIERS)]
        tail = jnp.where(place == 0, parts[0], jnp.where(place == 1, parts[1], parts[2]))
        buf[k, TAIL, at, :] = jnp.where(top, last, tail)
        for n, i in enumerate(SENT):
            value = planes[n]
            if i in FIXED_TOP:
                value = jnp.where(top, taken * jnp.float32(WEIGHTS[i]), value)
            buf[k, i, at, :] = value

    me = lax.axis_index("gx")
    copies = [pltpu.make_async_copy(buf.at[k], out_hbm.at[0, k], sem.at[k]) for k in range(CAP)]
    for k in range(CAP):
        taken = (table_ref[me * CAP + k] >= 0).astype(f32)
        for t in range(4):
            slot(k, taken, t)
        copies[k].start()
    for copy in copies:
        copy.wait()


def restore(table, arrived):
    return pl.pallas_call(
        restore_kernel,
        in_specs=[SMEM_SPEC, VMEM_SPEC],
        out_specs=HBM_SPEC,
        out_shape=jax.ShapeDtypeStruct((1, CAP, Q, B, LANES), f32),
        scratch_shapes=[pltpu.VMEM((CAP, Q, B, LANES), f32), pltpu.SemaphoreType.DMA((CAP,))],
        compiler_params=params(),
        name="restore",
    )(table, arrived)


def block_codes():
    codes = []
    for b in range(NDEV * BLK):
        s, j = divmod(b, BLK)
        edge = j % BXD == BXD - 1
        ns, nj = ((s + 1) % NDEV, j - BXD + 1) if edge else (s, j + 1)
        codes.append(s + (j << 4) + (ns << 8) + (nj << 12))
    return np.array(codes, np.int32)


def tables(owner, gy):
    flat = lax.dynamic_index_in_dim(owner, gy, 0, keepdims=False).reshape(-1)
    number = jnp.arange(NDEV * BLK)
    same = (flat[:, None] == flat[None, :]) & (number[None, :] < number[:, None])
    slot = jnp.sum(same.astype(i32), axis=1)
    target = jnp.where(flat >= 0, flat * CAP + slot, -1)
    hit = target[:, None] == jnp.arange(NDEV * CAP)[None, :]
    return jnp.max(jnp.where(hit, block_codes()[:, None], -1), axis=0).astype(i32)


def local(populations, heights, wall_class, wetting, owner):
    gy = lax.axis_index("gy")
    n_gy = lax.axis_size("gy")
    left = lax.ppermute(pack_cols(populations), "gx", [(i, (i + 1) % NDEV) for i in range(NDEV)])
    own, gas, packed, up, down = own_part(
        owner.transpose(2, 0, 1), wetting, populations, heights, wall_class
    )
    up, down = pack_rows(up, down, left)
    up, owner = lax.optimization_barrier((up, owner))
    below = lax.ppermute(up, "gy", [(i, (i - 1) % n_gy) for i in range(n_gy)])
    above = lax.ppermute(down, "gy", [(i, (i + 1) % n_gy) for i in range(n_gy)])
    table = tables(owner, gy)
    post, two, halves, message = inner_part(own, gas, packed, left)
    message = edge_part(table, message, halves, own, post, two, gas, below, above)
    gathered = lax.all_to_all(message, "gx", split_axis=0, concat_axis=0, tiled=True)
    chosen = sort_blocks(table, gathered)
    arrived = lax.all_to_all(chosen, "gx", split_axis=0, concat_axis=0, tiled=True)
    return restore(table, arrived)


def solution(mesh):
    return jax.shard_map(
        local,
        mesh=mesh,
        in_specs=(P(None, "gy", "gx"), P(), P(), P(), P()),
        out_specs=P("gy", "gx", None, None, None),
        check_vma=False,
    )
```

```python
import functools

import jax
import jax.numpy as jnp
import numpy as np
from jax import lax
from jax.experimental import pallas as pl
from jax.experimental.pallas import tpu as pltpu
from jax.sharding import PartitionSpec as P

B = 32
CZ = 4
BXD = 3
BYD = 2
CAP = 4
NCLS = 4
BLK = BXD * BYD
Q = 19
TILE = 8
LANES = 128
ROWS = 64
GROUPS = ROWS // TILE
SENT = [i for i in range(Q) if i != 17]
TAIL = 17
NDEV = 16
PIECE = BLK * (B + 4)
SLOTS = CAP * (B + 4)

VELOCITY = [
    (0, 0, 0),
    (1, 0, 0),
    (-1, 0, 0),
    (0, 1, 0),
    (0, -1, 0),
    (0, 0, 1),
    (0, 0, -1),
    (1, 1, 0),
    (-1, -1, 0),
    (1, -1, 0),
    (-1, 1, 0),
    (1, 0, 1),
    (-1, 0, -1),
    (1, 0, -1),
    (-1, 0, 1),
    (0, 1, 1),
    (0, -1, -1),
    (0, 1, -1),
    (0, -1, 1),
]
WEIGHTS = [1.0 / 3.0] + [1.0 / 18.0] * 6 + [1.0 / 36.0] * 12
OPPOSITE = [0, 2, 1, 4, 3, 6, 5, 8, 7, 10, 9, 12, 11, 14, 13, 16, 15, 18, 17]
CARRIERS = (6, 12, 13)
FIXED_TOP = (6, 12, 13, 16)

f32 = jnp.float32
i32 = jnp.int32
MIB = 1024 * 1024
PACK_LIMIT = 52 * MIB
OWN_LIMIT = 50 * MIB


def params(limit=16 * MIB):
    return pltpu.CompilerParams(vmem_limit_bytes=limit)


VMEM_SPEC = pl.BlockSpec(memory_space=pltpu.VMEM)
HBM_SPEC = pl.BlockSpec(memory_space=pltpu.HBM)
SMEM_SPEC = pl.BlockSpec(memory_space=pltpu.SMEM)
OWN_SHAPE = jax.ShapeDtypeStruct((Q, 3, ROWS, LANES), f32)
TWO_SHAPE = jax.ShapeDtypeStruct((Q, 4, ROWS, LANES), f32)
LEFT_SHAPE = jax.ShapeDtypeStruct((Q, ROWS, LANES), f32)
EDGE_SHAPE = jax.ShapeDtypeStruct((2 * Q + 2, 4 * LANES), f32)
MESSAGE_SHAPE = jax.ShapeDtypeStruct((NDEV, PIECE, LANES), f32)
HALVES_SHAPE = jax.ShapeDtypeStruct((NDEV, 4 * BLK, LANES), f32)


def lane_of():
    return lax.broadcasted_iota(i32, (TILE, LANES), 1)


def row_of():
    return lax.broadcasted_iota(i32, (TILE, LANES), 0)


def collide(f, gas):
    pairs = [(i, i + 1) for i in range(1, Q, 2)]
    total = {i: f[i] + f[o] for i, o in pairs}
    diff = {i: f[i] - f[o] for i, o in pairs}
    rho = f[0]
    for i, _ in pairs:
        rho = rho + total[i]
    jx = diff[1] + diff[7] + diff[9] + diff[11] + diff[13]
    jy = diff[3] + diff[7] - diff[9] + diff[15] + diff[17]
    jz = diff[5] + diff[11] - diff[13] + diff[15] - diff[17]
    inv = 1.0 / rho
    scaled = rho - 1.5 * inv * (jx * jx + jy * jy + jz * jz)
    along = {
        1: jx,
        3: jy,
        5: jz,
        7: jx + jy,
        9: jx - jy,
        11: jx + jz,
        13: jx - jz,
        15: jy + jz,
        17: jy - jz,
    }
    is_gas = gas > 0
    out = [None] * Q
    out[0] = jnp.where(
        is_gas, WEIGHTS[0] * gas, -0.6 * f[0] + (1.6 * WEIGHTS[0]) * scaled
    )
    for first, last in ((1, 5), (7, 17)):
        w = WEIGHTS[first]
        base = (1.6 * w) * scaled
        bend = (7.2 * w) * inv
        held = w * gas
        for i in range(first, last + 1, 2):
            cj = along[i]
            even = base + bend * (cj * cj) - 0.3 * total[i]
            odd = 0.25 * diff[i] + (1.5 * w) * cj
            out[i] = jnp.where(is_gas, held, even + odd)
            out[i + 1] = jnp.where(is_gas, held, even - odd)
    return out


def shifted(load, c, shift, lane):
    if shift == 0:
        return load(c)
    here = load(c)
    if shift > 0:
        if c != 3:
            here = jnp.where(lane >= LANES - shift, load((c + 3) % 4), here)
        return pltpu.roll(here, shift, 1)
    if c != 2:
        here = jnp.where(lane < -shift, load((c + 1) % 4), here)
    return pltpu.roll(here, LANES + shift, 1)


def shifted_message(load, c, shift, lane):
    if c != 2:
        return shifted(load, c, shift, lane)
    if shift == 0:
        return jnp.where(lane >= LANES - 8, load(3), load(2))
    if shift > 0:
        here = jnp.where(lane >= LANES - 8 - shift, load(3), load(2))
        here = jnp.where(lane >= LANES - shift, load(1), here)
        return pltpu.roll(here, shift, 1)
    here = jnp.where(lane >= LANES - 8 - shift, load(3), load(2))
    here = jnp.where(lane < -shift, load(0), here)
    return pltpu.roll(here, LANES + shift, 1)


def pull(load, i, c, lane, move=shifted):
    cx, cy, cz = VELOCITY[i]
    moved = move(lambda t: load(i, t, cy), c, 4 * cx + cz, lane)
    if cz == 1:
        wall = move(lambda t: load(OPPOSITE[i], t, 0), c, 0, lane)
        moved = jnp.where(lane % CZ == 0, wall, moved)
    elif cz == -1:
        moved = jnp.where(lane % CZ == CZ - 1, jnp.float32(WEIGHTS[i]), moved)
    return moved


def pack_cols_kernel(pop_hbm, out_ref, buf, sem):
    copies = []
    for g in range(GROUPS):
        rows = pl.ds(TILE * g, TILE)
        copies.append(
            pltpu.make_async_copy(
                pop_hbm.at[:, rows, pl.ds(2 * LANES, LANES)], buf.at[:, rows, :], sem.at[g]
            )
        )
        copies[-1].start()
    lane = lane_of()
    for copy in copies:
        copy.wait()
    for i in range(Q):
        packed = pltpu.roll(buf[i, 0:TILE, :], 16, 1)
        for g in range(1, GROUPS):
            last = buf[i, TILE * g : TILE * (g + 1), :]
            if g < GROUPS - 1:
                last = pltpu.roll(last, 16 * (g + 1), 1)
            packed = jnp.where(lane >= 16 * g, last, packed)
        out_ref[i] = packed


def pack_cols(populations):
    return pl.pallas_call(
        pack_cols_kernel,
        in_specs=[HBM_SPEC],
        out_specs=VMEM_SPEC,
        out_shape=jax.ShapeDtypeStruct((Q, TILE, LANES), f32),
        scratch_shapes=[pltpu.VMEM((Q, ROWS, LANES), f32), pltpu.SemaphoreType.DMA((GROUPS,))],
        compiler_params=params(PACK_LIMIT),
        name="pack_cols",
    )(populations)


def own_kernel(
    owner_ref,
    wet_ref,
    pop_hbm,
    height_hbm,
    kind_hbm,
    post_ref,
    gas_ref,
    packed_ref,
    up_ref,
    down_ref,
    pop,
    height,
    kind,
    pop_sem,
    field_sem,
):
    gy, gx = (lax.axis_index("gy"), lax.axis_index("gx"))
    n_gy = height_hbm.shape[1] // ROWS
    n_x = height_hbm.shape[2] // LANES
    start = lax.rem(gx * (BXD * B) + n_x * LANES - 4, n_x * LANES)
    first = start // LANES
    offset = start - first * LANES
    second = lax.rem(first + 1, n_x)
    up_gy, down_gy = (lax.rem(gy + n_gy - 1, n_gy), lax.rem(gy + 1, n_gy))
    copies = []
    for half, col in enumerate((first, second)):
        cols = pl.ds(pl.multiple_of(col * LANES, LANES), LANES)
        to = pl.ds(LANES * half, LANES)
        for row, at, count in (
            (gy * ROWS, TILE, ROWS),
            (up_gy * ROWS + ROWS - TILE, 0, TILE),
            (down_gy * ROWS, TILE + ROWS, TILE),
        ):
            rows = pl.ds(pl.multiple_of(row, TILE), count)
            n = len(copies)
            copies.append(
                pltpu.make_async_copy(
                    height_hbm.at[:, rows, cols], height.at[:, pl.ds(at, count), to], field_sem.at[n]
                )
            )
            copies.append(
                pltpu.make_async_copy(
                    kind_hbm.at[rows, cols], kind.at[pl.ds(at, count), to], field_sem.at[n + 1]
                )
            )
    for copy in copies:
        copy.start()

    def pop_copy(g):
        rows = pl.ds(pl.multiple_of(TILE * g, TILE), TILE)
        return pltpu.make_async_copy(pop_hbm.at[:, rows, :], pop.at[:, rows, :], pop_sem.at[g])

    for g in range(GROUPS):
        pop_copy(g).start()

    wide = 4 * LANES
    cell = lax.broadcasted_iota(i32, (2 * LANES, wide), 0)
    place = lax.broadcasted_iota(i32, (2 * LANES, wide), 1)
    spread = (cell == offset + 4 + place // CZ - jnp.where(place >= 3 * LANES, LANES, 0)).astype(f32)

    def widen(values):
        return jnp.dot(values.astype(f32), spread, preferred_element_type=f32)

    def active(row, col, j):
        return (owner_ref[j, row, col] >= 0).astype(f32)

    left_gx = lax.rem(gx + NDEV - 1, NDEV)

    def act_tile(row, by, c):
        return active(row, gx, BXD * by + c) if c < 3 else active(row, left_gx, BXD * by + 2)

    for copy in copies:
        copy.wait()
    kinds = widen(kind[...])
    value = wet_ref[0]
    for n in range(1, NCLS):
        value = jnp.where(kinds > n - 0.5, wet_ref[n], value)
    level = 1.0 + value
    lane = lane_of()
    depth = (lane % CZ).astype(f32)
    sub_low = row_of() < 4
    low, high = (TILE + ROWS, 0)
    for s in range(2):
        tall = widen(height[s])
        for c in range(4):
            cols = slice(LANES * c, LANES * (c + 1))
            for by in range(BYD):
                act = act_tile(gy, by, c)
                for rr in range(4):
                    g = 4 * by + rr
                    rows = slice(TILE * (g + 1), TILE * (g + 2))
                    fluid = depth < tall[rows, cols] * act
                    gas_ref[s, g, c] = jnp.where(fluid, 0.0, level[rows, cols])
            act = jnp.where(sub_low, act_tile(down_gy, 0, c), act_tile(up_gy, 1, c))
            here = jnp.where(sub_low, tall[low : low + TILE, cols], tall[high : high + TILE, cols])
            wall = jnp.where(sub_low, level[low : low + TILE, cols], level[high : high + TILE, cols])
            gas_ref[s, GROUPS, c] = jnp.where(depth < here * act, 0.0, wall)
    packed = pltpu.roll(gas_ref[0, 0, 3], 16, 1)
    for g in range(1, GROUPS):
        tile = gas_ref[0, g, 3]
        if g < GROUPS - 1:
            tile = pltpu.roll(tile, 16 * (g + 1), 1)
        packed = jnp.where(lane >= 16 * g, tile, packed)
    packed_ref[...] = packed

    def step(g, carry):
        pop_copy(g).wait()
        rows = pl.ds(pl.multiple_of(TILE * g, TILE), TILE)
        for c in range(3):
            f = [pop[i, rows, LANES * c : LANES * (c + 1)] for i in range(Q)]
            out = collide(f, gas_ref[0, g, c])
            for i in range(Q):
                post_ref[i, c, rows, :] = out[i]
        return carry

    lax.fori_loop(0, GROUPS, step, 0)
    for i in range(Q):
        up_ref[2 * i : 2 * i + 2, :] = pop[i, 0:2, :]
        down_ref[2 * i : 2 * i + 2, :] = pop[i, ROWS - 2 : ROWS, :]


def own_part(owner, wetting, populations, heights, wall_class):
    return pl.pallas_call(
        own_kernel,
        in_specs=[SMEM_SPEC, SMEM_SPEC, HBM_SPEC, HBM_SPEC, HBM_SPEC],
        out_specs=[VMEM_SPEC] * 5,
        out_shape=[
            OWN_SHAPE,
            jax.ShapeDtypeStruct((2, GROUPS + 1, 4, TILE, LANES), f32),
            jax.ShapeDtypeStruct((TILE, LANES), f32),
            jax.ShapeDtypeStruct((2 * Q + 2, 3 * LANES), f32),
            jax.ShapeDtypeStruct((2 * Q + 2, 3 * LANES), f32),
        ],
        scratch_shapes=[
            pltpu.VMEM((Q, ROWS, 3 * LANES), f32),
            pltpu.VMEM((2, ROWS + 2 * TILE, 2 * LANES), i32),
            pltpu.VMEM((ROWS + 2 * TILE, 2 * LANES), i32),
            pltpu.SemaphoreType.DMA((GROUPS,)),
            pltpu.SemaphoreType.DMA((12,)),
        ],
        compiler_params=params(OWN_LIMIT),
        cost_estimate=pl.CostEstimate(flops=8_000_000, bytes_accessed=8_000_000, transcendentals=0),
        name="own_cells",
    )(owner, wetting, populations, heights, wall_class)


def pack_rows_kernel(up_in, down_in, left_ref, up_ref, down_ref):
    up_ref[:, 0 : 3 * LANES] = up_in[...]
    down_ref[:, 0 : 3 * LANES] = down_in[...]
    for i in range(Q):
        first = pltpu.roll(left_ref[i], LANES - 16, 1)
        up_ref[2 * i : 2 * i + 2, 3 * LANES :] = first[0:2]
        down_ref[2 * i : 2 * i + 2, 3 * LANES :] = left_ref[i, TILE - 2 : TILE, :]


def pack_rows(up, down, left):
    return pl.pallas_call(
        pack_rows_kernel,
        in_specs=[VMEM_SPEC] * 3,
        out_specs=[VMEM_SPEC] * 2,
        out_shape=[EDGE_SHAPE, EDGE_SHAPE],
        compiler_params=params(),
        name="pack_rows",
    )(up, down, left)


def store_running(load, out_ref, halves_ref, by, rr, lane):
    for c in range(3):
        j = BXD * by + c
        tail = pull(load, TAIL, c, lane, shifted_message)
        for n, i in enumerate(SENT):
            value = pull(load, i, c, lane, shifted_message)
            if i in CARRIERS:
                back = 3 - CARRIERS.index(i)
                value = jnp.where(lane % CZ == CZ - 1, pltpu.roll(tail, back, 1), value)
            if n < NDEV:
                out_ref[n, B * j + TILE * rr : B * j + TILE * (rr + 1), :] = value
            else:
                m = 8 * (n - NDEV) + 2 * rr
                halves_ref[m, 4 * j : 4 * j + 4, :] = value[0:4]
                halves_ref[m + 1, 4 * j : 4 * j + 4, :] = value[4:8]


INNER = ((0, 2), (0, 3), (1, 0), (1, 1))
OUTER = ((0, 0), (0, 1), (1, 2), (1, 3))


def message_copy(buf, out_hbm, sem, j, start):
    rows = pl.ds(B * j + start, 2 * TILE)
    return pltpu.make_async_copy(buf.at[:, rows, :], out_hbm.at[:, rows, :], sem.at[j])


def inner_kernel(own_ref, gas_ref, packed_ref, left_ref, post_ref, two_ref, halves_ref, out_hbm, buf, sem):
    lane = lane_of()
    out = collide([left_ref[i] for i in range(Q)], packed_ref[...])
    for i in range(Q):
        for g in range(GROUPS):
            tile = out[i] if g == GROUPS - 1 else pltpu.roll(out[i], LANES - 16 * (g + 1), 1)
            post_ref[i, TILE * g : TILE * (g + 1), :] = tile

    def second(g, carry):
        def load(i, c, dy):
            rows = pl.ds(TILE * g - dy, TILE)
            return own_ref[i, c, rows, :] if c < 3 else post_ref[i, rows, :]

        for c in range(4):
            out = collide([pull(load, i, c, lane) for i in range(Q)], gas_ref[1, g, c])
            for i in range(Q):
                two_ref[i, c, pl.ds(pl.multiple_of(TILE * g, TILE), TILE), :] = out[i]
        return carry

    lax.fori_loop(1, GROUPS - 1, second, 0)
    copies = []
    for by, rr in INNER:
        at = TILE * (4 * by + rr)
        store_running(
            lambda i, c, dy: two_ref[i, c, at - dy : at - dy + TILE, :], buf, halves_ref, by, rr, lane
        )
        if rr % 2 == 1:
            for c in range(3):
                copies.append(message_copy(buf, out_hbm, sem, BXD * by + c, TILE * (rr - 1)))
                copies[-1].start()
    for copy in copies:
        copy.wait()


def inner_part(own, gas, packed, left):
    return pl.pallas_call(
        inner_kernel,
        in_specs=[VMEM_SPEC] * 4,
        out_specs=[VMEM_SPEC, VMEM_SPEC, VMEM_SPEC, HBM_SPEC],
        out_shape=[LEFT_SHAPE, TWO_SHAPE, HALVES_SHAPE, MESSAGE_SHAPE],
        scratch_shapes=[pltpu.VMEM((NDEV, BLK * B, LANES), f32), pltpu.SemaphoreType.DMA((BLK,))],
        compiler_params=params(),
        cost_estimate=pl.CostEstimate(flops=8_000_000, bytes_accessed=8_000_000, transcendentals=0),
        name="inner_rows",
    )(own, gas, packed, left)


def edge_kernel(
    table_ref,
    message_in,
    halves_in,
    own_ref,
    post_ref,
    two_ref,
    gas_ref,
    below_ref,
    above_ref,
    out_hbm,
    halo,
    top,
    bottom,
    top_two,
    bottom_two,
    buf,
    halves,
    sem,
    half_sem,
):
    lane = lane_of()
    sub_low = row_of() < 4
    tall = ROWS - TILE

    halves[...] = halves_in[...]
    halo[...] = jnp.ones(halo.shape, f32)
    for i in range(Q):
        for c in range(4):
            cols = slice(LANES * c, LANES * (c + 1))
            halo[i, c, 0:2, :] = below_ref[2 * i : 2 * i + 2, cols]
            halo[i, c, TILE - 2 : TILE, :] = above_ref[2 * i : 2 * i + 2, cols]
            first = own_ref[i, c, 0:TILE, :] if c < 3 else post_ref[i, 0:TILE, :]
            last = own_ref[i, c, tall:ROWS, :] if c < 3 else post_ref[i, tall:ROWS, :]
            top[i, c, 16:24, :] = first
            bottom[i, c, 8:16, :] = last
            top_two[i, c, 24:32, :] = two_ref[i, c, TILE : 2 * TILE, :]
            bottom_two[i, c, 8:16, :] = two_ref[i, c, tall - TILE : tall, :]
    for c in range(4):
        out = collide([halo[i, c] for i in range(Q)], gas_ref[0, GROUPS, c])
        for i in range(Q):
            top[i, c, 8:16, :] = out[i]
            bottom[i, c, 16:24, :] = out[i]

    def load_first(i, c, dy):
        if dy == 1:
            return top[i, c, 15:23, :]
        return own_ref[i, c, -dy : TILE - dy, :] if c < 3 else post_ref[i, -dy : TILE - dy, :]

    def load_last(i, c, dy):
        if dy == -1:
            return bottom[i, c, 9:17, :]
        return own_ref[i, c, tall - dy : ROWS - dy, :] if c < 3 else post_ref[i, tall - dy : ROWS - dy, :]

    def load_halo(i, c, dy):
        return jnp.where(sub_low, bottom[i, c, 16 - dy : 24 - dy, :], top[i, c, 8 - dy : 16 - dy, :])

    for c in range(4):
        out = collide([pull(load_first, i, c, lane) for i in range(Q)], gas_ref[1, 0, c])
        for i in range(Q):
            top_two[i, c, 16:24, :] = out[i]
        out = collide([pull(load_last, i, c, lane) for i in range(Q)], gas_ref[1, GROUPS - 1, c])
        for i in range(Q):
            bottom_two[i, c, 16:24, :] = out[i]
        out = collide([pull(load_halo, i, c, lane) for i in range(Q)], gas_ref[1, GROUPS, c])
        for i in range(Q):
            top_two[i, c, 8:16, :] = out[i]
            bottom_two[i, c, 24:32, :] = out[i]

    copies = []
    for by, rr in OUTER:
        g = 4 * by + rr

        def load(i, c, dy):
            if by == 0 and (g == 0 or dy == 1):
                return top_two[i, c, 16 + TILE * g - dy : 24 + TILE * g - dy, :]
            if by == 1 and (g == GROUPS - 1 or dy == -1):
                at = TILE * (g - GROUPS + 3) - dy
                return bottom_two[i, c, at : at + TILE, :]
            return two_ref[i, c, TILE * g - dy : TILE * (g + 1) - dy, :]

        store_running(load, buf, halves, by, rr, lane)
        if rr % 2 == 1:
            for c in range(3):
                copies.append(message_copy(buf, out_hbm, sem, BXD * by + c, TILE * (rr - 1)))
                copies[-1].start()
    copies.append(
        pltpu.make_async_copy(halves, out_hbm.at[:, pl.ds(BLK * B, 4 * BLK), :], half_sem)
    )
    copies[-1].start()
    for copy in copies:
        copy.wait()


def edge_part(table, message, halves, own, post, two, gas, below, above):
    return pl.pallas_call(
        edge_kernel,
        in_specs=[SMEM_SPEC, HBM_SPEC] + [VMEM_SPEC] * 7,
        out_specs=HBM_SPEC,
        out_shape=MESSAGE_SHAPE,
        input_output_aliases={1: 0},
        scratch_shapes=[
            pltpu.VMEM((Q, 4, TILE, LANES), f32),
            pltpu.VMEM((Q, 4, 3 * TILE, LANES), f32),
            pltpu.VMEM((Q, 4, 4 * TILE, LANES), f32),
            pltpu.VMEM((Q, 4, 4 * TILE, LANES), f32),
            pltpu.VMEM((Q, 4, 4 * TILE, LANES), f32),
            pltpu.VMEM((NDEV, BLK * B, LANES), f32),
            pltpu.VMEM((NDEV, 4 * BLK, LANES), f32),
            pltpu.SemaphoreType.DMA((BLK,)),
            pltpu.SemaphoreType.DMA,
        ],
        compiler_params=params(),
        cost_estimate=pl.CostEstimate(flops=8_000_000, bytes_accessed=8_000_000, transcendentals=0),
        name="edge_rows",
    )(table, message, halves, own, post, two, gas, below, above)


def sort_kernel(table_ref, in_ref, out_ref):
    lane = lane_of()
    sub_low = row_of() < 4

    def receiver(d, carry):
        halves = []
        for k in range(CAP):
            code = table_ref[d * CAP + k]
            valid = code >= 0
            code = jnp.maximum(code, 0)
            s, j, after_s = (code & 15, (code >> 4) & 7, code >> 8)
            for t in range(4):
                rows = pl.ds(pl.multiple_of(B * j + TILE * t, TILE), TILE)
                tile = jnp.where(lane >= LANES - 8, in_ref[after_s, rows, :], in_ref[s, rows, :])
                out_ref[d, B * k + TILE * t : B * k + TILE * (t + 1), :] = jnp.where(valid, tile, 0.0)
            pair = lax.shift_right_logical(j, 1)
            rows = pl.ds(pl.multiple_of(BLK * B + TILE * pair, TILE), TILE)
            tile = jnp.where(lane >= LANES - 8, in_ref[after_s, rows, :], in_ref[s, rows, :])
            tile = jnp.where(j - 2 * pair == k % 2, tile, pltpu.roll(tile, 4, 0))
            halves.append(jnp.where(valid, tile, 0.0))
        for pair in range(CAP // 2):
            at = CAP * B + TILE * pair
            out_ref[d, at : at + TILE, :] = jnp.where(sub_low, halves[2 * pair], halves[2 * pair + 1])
        return carry

    lax.fori_loop(0, NDEV, receiver, 0, unroll=4)


def sort_blocks(table, arrived):
    return pl.pallas_call(
        sort_kernel,
        in_specs=[SMEM_SPEC, VMEM_SPEC],
        out_specs=VMEM_SPEC,
        out_shape=jax.ShapeDtypeStruct((NDEV, SLOTS, LANES), f32),
        compiler_params=params(),
        name="sort_blocks",
    )(table, arrived)


def restore_kernel(table_ref, in_ref, out_hbm, buf, sem):
    lane = lane_of()
    sub_low = row_of() < 4
    top = lane % CZ == CZ - 1
    place = lane % CZ

    def slot(k, taken, t):
        rows = slice(B * k + TILE * t, B * k + TILE * (t + 1))
        planes = {m: in_ref[m, rows, :] for m in range(NDEV)}
        pair = CAP * B + TILE * (k // 2)
        for p in range(2):
            a = in_ref[8 * p + 2 * t, pair : pair + TILE, :]
            b = in_ref[8 * p + 2 * t + 1, pair : pair + TILE, :]
            if k % 2 == 0:
                b = pltpu.roll(b, 4, 0)
            else:
                a = pltpu.roll(a, 4, 0)
            planes[NDEV + p] = jnp.where(sub_low, a, b)
        at = slice(TILE * t, TILE * (t + 1))
        last = taken * jnp.float32(WEIGHTS[TAIL])
        parts = [pltpu.roll(planes[i], LANES - 3 + n, 1) for n, i in enumerate(CARRIERS)]
        tail = jnp.where(place == 0, parts[0], jnp.where(place == 1, parts[1], parts[2]))
        buf[k, TAIL, at, :] = jnp.where(top, last, tail)
        for n, i in enumerate(SENT):
            value = planes[n]
            if i in FIXED_TOP:
                value = jnp.where(top, taken * jnp.float32(WEIGHTS[i]), value)
            buf[k, i, at, :] = value

    me = lax.axis_index("gx")
    copies = [pltpu.make_async_copy(buf.at[k], out_hbm.at[0, k], sem.at[k]) for k in range(CAP)]
    for k in range(CAP):
        taken = (table_ref[me * CAP + k] >= 0).astype(f32)
        for t in range(4):
            slot(k, taken, t)
        copies[k].start()
    for copy in copies:
        copy.wait()


def restore(table, arrived):
    return pl.pallas_call(
        restore_kernel,
        in_specs=[SMEM_SPEC, VMEM_SPEC],
        out_specs=HBM_SPEC,
        out_shape=jax.ShapeDtypeStruct((1, CAP, Q, B, LANES), f32),
        scratch_shapes=[pltpu.VMEM((CAP, Q, B, LANES), f32), pltpu.SemaphoreType.DMA((CAP,))],
        compiler_params=params(),
        name="restore",
    )(table, arrived)


def block_codes():
    codes = []
    for b in range(NDEV * BLK):
        s, j = divmod(b, BLK)
        after = (s + 1) % NDEV if j % BXD == BXD - 1 else s
        codes.append(s + (j << 4) + (after << 8))
    return np.array(codes, np.int32)


def tables(owner, gy):
    flat = lax.dynamic_index_in_dim(owner, gy, 0, keepdims=False).reshape(-1)
    number = jnp.arange(NDEV * BLK)
    same = (flat[:, None] == flat[None, :]) & (number[None, :] < number[:, None])
    slot = jnp.sum(same.astype(i32), axis=1)
    target = jnp.where(flat >= 0, flat * CAP + slot, -1)
    hit = target[:, None] == jnp.arange(NDEV * CAP)[None, :]
    return jnp.max(jnp.where(hit, block_codes()[:, None], -1), axis=0).astype(i32)


def local(populations, heights, wall_class, wetting, owner):
    gy = lax.axis_index("gy")
    n_gy = lax.axis_size("gy")
    left = lax.ppermute(pack_cols(populations), "gx", [(i, (i + 1) % NDEV) for i in range(NDEV)])
    own, gas, packed, up, down = own_part(
        owner.transpose(2, 0, 1), wetting, populations, heights, wall_class
    )
    up, down = pack_rows(up, down, left)
    up, owner = lax.optimization_barrier((up, owner))
    below = lax.ppermute(up, "gy", [(i, (i - 1) % n_gy) for i in range(n_gy)])
    above = lax.ppermute(down, "gy", [(i, (i + 1) % n_gy) for i in range(n_gy)])
    table = tables(owner, gy)
    post, two, halves, message = inner_part(own, gas, packed, left)
    message = edge_part(table, message, halves, own, post, two, gas, below, above)
    gathered = lax.all_to_all(message, "gx", split_axis=0, concat_axis=0, tiled=True)
    chosen = sort_blocks(table, gathered)
    arrived = lax.all_to_all(chosen, "gx", split_axis=0, concat_axis=0, tiled=True)
    return restore(table, arrived)


def solution(mesh):
    return jax.shard_map(
        local,
        mesh=mesh,
        in_specs=(P(None, "gy", "gx"), P(), P(), P(), P()),
        out_specs=P("gy", "gx", None, None, None),
        check_vma=False,
    )
```

```python
import functools

import jax
import jax.numpy as jnp
import numpy as np
from jax import lax
from jax.experimental import pallas as pl
from jax.experimental.pallas import tpu as pltpu
from jax.sharding import PartitionSpec as P

B = 32
CZ = 4
BXD = 3
BYD = 2
CAP = 4
NCLS = 4
BLK = BXD * BYD
Q = 19
TILE = 8
LANES = 128
ROWS = 64
GROUPS = ROWS // TILE
SENT = [i for i in range(Q) if i != 17]
TAIL = 17
NDEV = 16
PIECE = BLK * (B + 4)
SLOTS = CAP * (B + 4)

VELOCITY = [
    (0, 0, 0),
    (1, 0, 0),
    (-1, 0, 0),
    (0, 1, 0),
    (0, -1, 0),
    (0, 0, 1),
    (0, 0, -1),
    (1, 1, 0),
    (-1, -1, 0),
    (1, -1, 0),
    (-1, 1, 0),
    (1, 0, 1),
    (-1, 0, -1),
    (1, 0, -1),
    (-1, 0, 1),
    (0, 1, 1),
    (0, -1, -1),
    (0, 1, -1),
    (0, -1, 1),
]
WEIGHTS = [1.0 / 3.0] + [1.0 / 18.0] * 6 + [1.0 / 36.0] * 12
OPPOSITE = [0, 2, 1, 4, 3, 6, 5, 8, 7, 10, 9, 12, 11, 14, 13, 16, 15, 18, 17]
CARRIERS = (6, 12, 13)

f32 = jnp.float32
i32 = jnp.int32
MIB = 1024 * 1024
PACK_LIMIT = 52 * MIB
OWN_LIMIT = 50 * MIB


def params(limit=16 * MIB):
    return pltpu.CompilerParams(vmem_limit_bytes=limit)


VMEM_SPEC = pl.BlockSpec(memory_space=pltpu.VMEM)
HBM_SPEC = pl.BlockSpec(memory_space=pltpu.HBM)
SMEM_SPEC = pl.BlockSpec(memory_space=pltpu.SMEM)
OWN_SHAPE = jax.ShapeDtypeStruct((Q, 3, ROWS, LANES), f32)
TWO_SHAPE = jax.ShapeDtypeStruct((Q, 4, ROWS, LANES), f32)
LEFT_SHAPE = jax.ShapeDtypeStruct((Q, ROWS, LANES), f32)
EDGE_SHAPE = jax.ShapeDtypeStruct((2 * Q + 2, 4 * LANES), f32)
MESSAGE_SHAPE = jax.ShapeDtypeStruct((NDEV, PIECE, LANES), f32)
PART_SHAPE = jax.ShapeDtypeStruct((NDEV, BLK * 2 * TILE, LANES), f32)
HALVES_SHAPE = jax.ShapeDtypeStruct((NDEV, 4 * BLK, LANES), f32)


def lane_of():
    return lax.broadcasted_iota(i32, (TILE, LANES), 1)


def row_of():
    return lax.broadcasted_iota(i32, (TILE, LANES), 0)


def collide(f, gas):
    pairs = [(i, i + 1) for i in range(1, Q, 2)]
    total = {i: f[i] + f[o] for i, o in pairs}
    diff = {i: f[i] - f[o] for i, o in pairs}
    rho = f[0]
    for i, _ in pairs:
        rho = rho + total[i]
    jx = diff[1] + diff[7] + diff[9] + diff[11] + diff[13]
    jy = diff[3] + diff[7] - diff[9] + diff[15] + diff[17]
    jz = diff[5] + diff[11] - diff[13] + diff[15] - diff[17]
    inv = 1.0 / rho
    scaled = rho - 1.5 * inv * (jx * jx + jy * jy + jz * jz)
    along = {
        1: jx,
        3: jy,
        5: jz,
        7: jx + jy,
        9: jx - jy,
        11: jx + jz,
        13: jx - jz,
        15: jy + jz,
        17: jy - jz,
    }
    is_gas = gas > 0
    out = [None] * Q
    out[0] = jnp.where(
        is_gas, WEIGHTS[0] * gas, -0.6 * f[0] + (1.6 * WEIGHTS[0]) * scaled
    )
    for first, last in ((1, 5), (7, 17)):
        w = WEIGHTS[first]
        base = (1.6 * w) * scaled
        bend = (7.2 * w) * inv
        held = w * gas
        for i in range(first, last + 1, 2):
            cj = along[i]
            even = base + bend * (cj * cj) - 0.3 * total[i]
            odd = 0.25 * diff[i] + (1.5 * w) * cj
            out[i] = jnp.where(is_gas, held, even + odd)
            out[i + 1] = jnp.where(is_gas, held, even - odd)
    return out


def shifted(load, c, shift, lane):
    if shift == 0:
        return load(c)
    here = load(c)
    if shift > 0:
        if c != 3:
            here = jnp.where(lane >= LANES - shift, load((c + 3) % 4), here)
        return pltpu.roll(here, shift, 1)
    if c != 2:
        here = jnp.where(lane < -shift, load((c + 1) % 4), here)
    return pltpu.roll(here, LANES + shift, 1)


def shifted_message(load, c, shift, lane):
    if c != 2:
        return shifted(load, c, shift, lane)
    if shift == 0:
        return jnp.where(lane >= LANES - 8, load(3), load(2))
    if shift > 0:
        here = jnp.where(lane >= LANES - 8 - shift, load(3), load(2))
        here = jnp.where(lane >= LANES - shift, load(1), here)
        return pltpu.roll(here, shift, 1)
    here = jnp.where(lane >= LANES - 8 - shift, load(3), load(2))
    here = jnp.where(lane < -shift, load(0), here)
    return pltpu.roll(here, LANES + shift, 1)


def pull(load, i, c, lane, move=shifted):
    cx, cy, cz = VELOCITY[i]
    moved = move(lambda t: load(i, t, cy), c, 4 * cx + cz, lane)
    if cz == 1:
        wall = move(lambda t: load(OPPOSITE[i], t, 0), c, 0, lane)
        moved = jnp.where(lane % CZ == 0, wall, moved)
    elif cz == -1:
        moved = jnp.where(lane % CZ == CZ - 1, jnp.float32(WEIGHTS[i]), moved)
    return moved


def pack_cols_kernel(pop_hbm, out_ref, buf, sem):
    copies = []
    for g in range(GROUPS):
        rows = pl.ds(TILE * g, TILE)
        copies.append(
            pltpu.make_async_copy(
                pop_hbm.at[:, rows, pl.ds(2 * LANES, LANES)], buf.at[:, rows, :], sem.at[g]
            )
        )
        copies[-1].start()
    lane = lane_of()
    for copy in copies:
        copy.wait()
    for i in range(Q):
        packed = pltpu.roll(buf[i, 0:TILE, :], 16, 1)
        for g in range(1, GROUPS):
            last = buf[i, TILE * g : TILE * (g + 1), :]
            if g < GROUPS - 1:
                last = pltpu.roll(last, 16 * (g + 1), 1)
            packed = jnp.where(lane >= 16 * g, last, packed)
        out_ref[i] = packed


def pack_cols(populations):
    return pl.pallas_call(
        pack_cols_kernel,
        in_specs=[HBM_SPEC],
        out_specs=VMEM_SPEC,
        out_shape=jax.ShapeDtypeStruct((Q, TILE, LANES), f32),
        scratch_shapes=[pltpu.VMEM((Q, ROWS, LANES), f32), pltpu.SemaphoreType.DMA((GROUPS,))],
        compiler_params=params(PACK_LIMIT),
        name="pack_cols",
    )(populations)


def own_kernel(
    owner_ref,
    wet_ref,
    pop_hbm,
    height_hbm,
    kind_hbm,
    post_ref,
    gas_ref,
    packed_ref,
    up_ref,
    down_ref,
    pop,
    height,
    kind,
    pop_sem,
    field_sem,
):
    gy, gx = (lax.axis_index("gy"), lax.axis_index("gx"))
    n_gy = height_hbm.shape[1] // ROWS
    n_x = height_hbm.shape[2] // LANES
    start = lax.rem(gx * (BXD * B) + n_x * LANES - 4, n_x * LANES)
    first = start // LANES
    offset = start - first * LANES
    second = lax.rem(first + 1, n_x)
    up_gy, down_gy = (lax.rem(gy + n_gy - 1, n_gy), lax.rem(gy + 1, n_gy))
    copies = []
    for half, col in enumerate((first, second)):
        cols = pl.ds(pl.multiple_of(col * LANES, LANES), LANES)
        to = pl.ds(LANES * half, LANES)
        for row, at, count in (
            (gy * ROWS, TILE, ROWS),
            (up_gy * ROWS + ROWS - TILE, 0, TILE),
            (down_gy * ROWS, TILE + ROWS, TILE),
        ):
            rows = pl.ds(pl.multiple_of(row, TILE), count)
            n = len(copies)
            copies.append(
                pltpu.make_async_copy(
                    height_hbm.at[:, rows, cols], height.at[:, pl.ds(at, count), to], field_sem.at[n]
                )
            )
            copies.append(
                pltpu.make_async_copy(
                    kind_hbm.at[rows, cols], kind.at[pl.ds(at, count), to], field_sem.at[n + 1]
                )
            )
    for copy in copies:
        copy.start()

    def pop_copy(g):
        rows = pl.ds(pl.multiple_of(TILE * g, TILE), TILE)
        return pltpu.make_async_copy(pop_hbm.at[:, rows, :], pop.at[:, rows, :], pop_sem.at[g])

    for g in range(GROUPS):
        pop_copy(g).start()

    wide = 4 * LANES
    cell = lax.broadcasted_iota(i32, (2 * LANES, wide), 0)
    place = lax.broadcasted_iota(i32, (2 * LANES, wide), 1)
    spread = (cell == offset + 4 + place // CZ - jnp.where(place >= 3 * LANES, LANES, 0)).astype(f32)

    def widen(values):
        return jnp.dot(values.astype(f32), spread, preferred_element_type=f32)

    def active(row, col, j):
        return (owner_ref[j, row, col] >= 0).astype(f32)

    left_gx = lax.rem(gx + NDEV - 1, NDEV)

    def act_tile(row, by, c):
        return active(row, gx, BXD * by + c) if c < 3 else active(row, left_gx, BXD * by + 2)

    for copy in copies:
        copy.wait()
    kinds = widen(kind[...])
    value = wet_ref[0]
    for n in range(1, NCLS):
        value = jnp.where(kinds > n - 0.5, wet_ref[n], value)
    level = 1.0 + value
    lane = lane_of()
    depth = (lane % CZ).astype(f32)
    sub_low = row_of() < 4
    low, high = (TILE + ROWS, 0)
    for s in range(2):
        tall = widen(height[s])
        for c in range(4):
            cols = slice(LANES * c, LANES * (c + 1))
            for by in range(BYD):
                act = act_tile(gy, by, c)
                for rr in range(4):
                    g = 4 * by + rr
                    rows = slice(TILE * (g + 1), TILE * (g + 2))
                    fluid = depth < tall[rows, cols] * act
                    gas_ref[s, g, c] = jnp.where(fluid, 0.0, level[rows, cols])
            act = jnp.where(sub_low, act_tile(down_gy, 0, c), act_tile(up_gy, 1, c))
            here = jnp.where(sub_low, tall[low : low + TILE, cols], tall[high : high + TILE, cols])
            wall = jnp.where(sub_low, level[low : low + TILE, cols], level[high : high + TILE, cols])
            gas_ref[s, GROUPS, c] = jnp.where(depth < here * act, 0.0, wall)
    packed = pltpu.roll(gas_ref[0, 0, 3], 16, 1)
    for g in range(1, GROUPS):
        tile = gas_ref[0, g, 3]
        if g < GROUPS - 1:
            tile = pltpu.roll(tile, 16 * (g + 1), 1)
        packed = jnp.where(lane >= 16 * g, tile, packed)
    packed_ref[...] = packed

    def step(g, carry):
        pop_copy(g).wait()
        rows = pl.ds(pl.multiple_of(TILE * g, TILE), TILE)
        for c in range(3):
            f = [pop[i, rows, LANES * c : LANES * (c + 1)] for i in range(Q)]
            out = collide(f, gas_ref[0, g, c])
            for i in range(Q):
                post_ref[i, c, rows, :] = out[i]
        return carry

    lax.fori_loop(0, GROUPS, step, 0)
    for i in range(Q):
        up_ref[2 * i : 2 * i + 2, :] = pop[i, 0:2, :]
        down_ref[2 * i : 2 * i + 2, :] = pop[i, ROWS - 2 : ROWS, :]


def own_part(owner, wetting, populations, heights, wall_class):
    return pl.pallas_call(
        own_kernel,
        in_specs=[SMEM_SPEC, SMEM_SPEC, HBM_SPEC, HBM_SPEC, HBM_SPEC],
        out_specs=[VMEM_SPEC] * 5,
        out_shape=[
            OWN_SHAPE,
            jax.ShapeDtypeStruct((2, GROUPS + 1, 4, TILE, LANES), f32),
            jax.ShapeDtypeStruct((TILE, LANES), f32),
            jax.ShapeDtypeStruct((2 * Q + 2, 3 * LANES), f32),
            jax.ShapeDtypeStruct((2 * Q + 2, 3 * LANES), f32),
        ],
        scratch_shapes=[
            pltpu.VMEM((Q, ROWS, 3 * LANES), f32),
            pltpu.VMEM((2, ROWS + 2 * TILE, 2 * LANES), i32),
            pltpu.VMEM((ROWS + 2 * TILE, 2 * LANES), i32),
            pltpu.SemaphoreType.DMA((GROUPS,)),
            pltpu.SemaphoreType.DMA((12,)),
        ],
        compiler_params=params(OWN_LIMIT),
        cost_estimate=pl.CostEstimate(flops=8_000_000, bytes_accessed=8_000_000, transcendentals=0),
        name="own_cells",
    )(owner, wetting, populations, heights, wall_class)


def pack_rows_kernel(up_in, down_in, left_ref, up_ref, down_ref):
    up_ref[:, 0 : 3 * LANES] = up_in[...]
    down_ref[:, 0 : 3 * LANES] = down_in[...]
    for i in range(Q):
        first = pltpu.roll(left_ref[i], LANES - 16, 1)
        up_ref[2 * i : 2 * i + 2, 3 * LANES :] = first[0:2]
        down_ref[2 * i : 2 * i + 2, 3 * LANES :] = left_ref[i, TILE - 2 : TILE, :]


def pack_rows(up, down, left):
    return pl.pallas_call(
        pack_rows_kernel,
        in_specs=[VMEM_SPEC] * 3,
        out_specs=[VMEM_SPEC] * 2,
        out_shape=[EDGE_SHAPE, EDGE_SHAPE],
        compiler_params=params(),
        name="pack_rows",
    )(up, down, left)


def store_running(load, out_ref, halves_ref, halves_at, by, rr, lane, start):
    for c in range(3):
        j = BXD * by + c
        tail = pull(load, TAIL, c, lane, shifted_message)
        for n, i in enumerate(SENT):
            value = pull(load, i, c, lane, shifted_message)
            if i in CARRIERS:
                back = 3 - CARRIERS.index(i)
                value = jnp.where(lane % CZ == CZ - 1, pltpu.roll(tail, back, 1), value)
            if n < NDEV:
                at = start(j) + TILE * (rr % 2)
                out_ref[n, at : at + TILE, :] = value
            else:
                m = 8 * (n - NDEV) + 2 * rr
                at = halves_at + 4 * j
                halves_ref[m, at : at + 4, :] = value[0:4]
                halves_ref[m + 1, at : at + 4, :] = value[4:8]


INNER = ((0, 2), (0, 3), (1, 0), (1, 1))
OUTER = ((0, 0), (0, 1), (1, 2), (1, 3))


def inner_kernel(own_ref, gas_ref, packed_ref, left_ref, post_ref, two_ref, halves_ref, part_ref):
    lane = lane_of()
    out = collide([left_ref[i] for i in range(Q)], packed_ref[...])
    for i in range(Q):
        for g in range(GROUPS):
            tile = out[i] if g == GROUPS - 1 else pltpu.roll(out[i], LANES - 16 * (g + 1), 1)
            post_ref[i, TILE * g : TILE * (g + 1), :] = tile

    def second(g, carry):
        def load(i, c, dy):
            rows = pl.ds(TILE * g - dy, TILE)
            return own_ref[i, c, rows, :] if c < 3 else post_ref[i, rows, :]

        for c in range(4):
            out = collide([pull(load, i, c, lane) for i in range(Q)], gas_ref[1, g, c])
            for i in range(Q):
                two_ref[i, c, pl.ds(pl.multiple_of(TILE * g, TILE), TILE), :] = out[i]
        return carry

    lax.fori_loop(1, GROUPS - 1, second, 0)
    for by, rr in INNER:
        at = TILE * (4 * by + rr)
        store_running(
            lambda i, c, dy: two_ref[i, c, at - dy : at - dy + TILE, :],
            part_ref,
            halves_ref,
            0,
            by,
            rr,
            lane,
            lambda j: 2 * TILE * j,
        )


def inner_part(own, gas, packed, left):
    return pl.pallas_call(
        inner_kernel,
        in_specs=[VMEM_SPEC] * 4,
        out_specs=[VMEM_SPEC] * 4,
        out_shape=[LEFT_SHAPE, TWO_SHAPE, HALVES_SHAPE, PART_SHAPE],
        compiler_params=params(),
        cost_estimate=pl.CostEstimate(flops=8_000_000, bytes_accessed=8_000_000, transcendentals=0),
        name="inner_rows",
    )(own, gas, packed, left)


def edge_kernel(
    part_ref,
    halves_ref,
    own_ref,
    post_ref,
    two_ref,
    gas_ref,
    below_ref,
    above_ref,
    out_ref,
    halo,
    top,
    bottom,
    top_two,
    bottom_two,
):
    lane = lane_of()
    sub_low = row_of() < 4
    tall = ROWS - TILE

    out_ref[:, BLK * B :, :] = halves_ref[...]
    for j in range(BLK):
        at = B * j + (2 * TILE if j < BXD else 0)
        out_ref[:, at : at + 2 * TILE, :] = part_ref[:, 2 * TILE * j : 2 * TILE * (j + 1), :]
    halo[...] = jnp.ones(halo.shape, f32)
    for i in range(Q):
        for c in range(4):
            cols = slice(LANES * c, LANES * (c + 1))
            halo[i, c, 0:2, :] = below_ref[2 * i : 2 * i + 2, cols]
            halo[i, c, TILE - 2 : TILE, :] = above_ref[2 * i : 2 * i + 2, cols]
            first = own_ref[i, c, 0:TILE, :] if c < 3 else post_ref[i, 0:TILE, :]
            last = own_ref[i, c, tall:ROWS, :] if c < 3 else post_ref[i, tall:ROWS, :]
            top[i, c, 16:24, :] = first
            bottom[i, c, 8:16, :] = last
            top_two[i, c, 24:32, :] = two_ref[i, c, TILE : 2 * TILE, :]
            bottom_two[i, c, 8:16, :] = two_ref[i, c, tall - TILE : tall, :]
    for c in range(4):
        out = collide([halo[i, c] for i in range(Q)], gas_ref[0, GROUPS, c])
        for i in range(Q):
            top[i, c, 8:16, :] = out[i]
            bottom[i, c, 16:24, :] = out[i]

    def load_first(i, c, dy):
        if dy == 1:
            return top[i, c, 15:23, :]
        return own_ref[i, c, -dy : TILE - dy, :] if c < 3 else post_ref[i, -dy : TILE - dy, :]

    def load_last(i, c, dy):
        if dy == -1:
            return bottom[i, c, 9:17, :]
        return own_ref[i, c, tall - dy : ROWS - dy, :] if c < 3 else post_ref[i, tall - dy : ROWS - dy, :]

    def load_halo(i, c, dy):
        return jnp.where(sub_low, bottom[i, c, 16 - dy : 24 - dy, :], top[i, c, 8 - dy : 16 - dy, :])

    for c in range(4):
        out = collide([pull(load_first, i, c, lane) for i in range(Q)], gas_ref[1, 0, c])
        for i in range(Q):
            top_two[i, c, 16:24, :] = out[i]
        out = collide([pull(load_last, i, c, lane) for i in range(Q)], gas_ref[1, GROUPS - 1, c])
        for i in range(Q):
            bottom_two[i, c, 16:24, :] = out[i]
        out = collide([pull(load_halo, i, c, lane) for i in range(Q)], gas_ref[1, GROUPS, c])
        for i in range(Q):
            top_two[i, c, 8:16, :] = out[i]
            bottom_two[i, c, 24:32, :] = out[i]

    for by, rr in OUTER:
        g = 4 * by + rr

        def load(i, c, dy):
            if by == 0 and (g == 0 or dy == 1):
                return top_two[i, c, 16 + TILE * g - dy : 24 + TILE * g - dy, :]
            if by == 1 and (g == GROUPS - 1 or dy == -1):
                at = TILE * (g - GROUPS + 3) - dy
                return bottom_two[i, c, at : at + TILE, :]
            return two_ref[i, c, TILE * g - dy : TILE * (g + 1) - dy, :]

        store_running(
            load, out_ref, out_ref, BLK * B, by, rr, lane, lambda j: B * j + 2 * TILE * (rr // 2)
        )


def edge_part(part, halves, own, post, two, gas, below, above):
    return pl.pallas_call(
        edge_kernel,
        in_specs=[VMEM_SPEC] * 8,
        out_specs=VMEM_SPEC,
        out_shape=MESSAGE_SHAPE,
        scratch_shapes=[
            pltpu.VMEM((Q, 4, TILE, LANES), f32),
            pltpu.VMEM((Q, 4, 3 * TILE, LANES), f32),
            pltpu.VMEM((Q, 4, 4 * TILE, LANES), f32),
            pltpu.VMEM((Q, 4, 4 * TILE, LANES), f32),
            pltpu.VMEM((Q, 4, 4 * TILE, LANES), f32),
        ],
        compiler_params=params(),
        cost_estimate=pl.CostEstimate(flops=8_000_000, bytes_accessed=8_000_000, transcendentals=0),
        name="edge_rows",
    )(part, halves, own, post, two, gas, below, above)


def sort_kernel(table_ref, in_ref, out_ref):
    lane = lane_of()
    sub_low = row_of() < 4

    def receiver(d, carry):
        halves = []
        for k in range(CAP):
            code = table_ref[d * CAP + k]
            valid = code >= 0
            code = jnp.maximum(code, 0)
            s, j, after_s = (code & 15, (code >> 4) & 7, code >> 8)
            for t in range(4):
                rows = pl.ds(pl.multiple_of(B * j + TILE * t, TILE), TILE)
                tile = jnp.where(lane >= LANES - 8, in_ref[after_s, rows, :], in_ref[s, rows, :])
                out_ref[d, B * k + TILE * t : B * k + TILE * (t + 1), :] = jnp.where(valid, tile, 0.0)
            pair = lax.shift_right_logical(j, 1)
            rows = pl.ds(pl.multiple_of(BLK * B + TILE * pair, TILE), TILE)
            tile = jnp.where(lane >= LANES - 8, in_ref[after_s, rows, :], in_ref[s, rows, :])
            tile = jnp.where(j - 2 * pair == k % 2, tile, pltpu.roll(tile, 4, 0))
            halves.append(jnp.where(valid, tile, 0.0))
        for pair in range(CAP // 2):
            at = CAP * B + TILE * pair
            out_ref[d, at : at + TILE, :] = jnp.where(sub_low, halves[2 * pair], halves[2 * pair + 1])
        return carry

    lax.fori_loop(0, NDEV, receiver, 0, unroll=4)


def sort_blocks(table, arrived):
    return pl.pallas_call(
        sort_kernel,
        in_specs=[SMEM_SPEC, VMEM_SPEC],
        out_specs=VMEM_SPEC,
        out_shape=jax.ShapeDtypeStruct((NDEV, SLOTS, LANES), f32),
        compiler_params=params(),
        name="sort_blocks",
    )(table, arrived)


def restore_kernel(in_ref, out_hbm, buf, sem):
    lane = lane_of()
    sub_low = row_of() < 4
    top = lane % CZ == CZ - 1
    place = lane % CZ

    def slot(k, t):
        rows = slice(B * k + TILE * t, B * k + TILE * (t + 1))
        planes = {m: in_ref[m, rows, :] for m in range(NDEV)}
        pair = CAP * B + TILE * (k // 2)
        for p in range(2):
            a = in_ref[8 * p + 2 * t, pair : pair + TILE, :]
            b = in_ref[8 * p + 2 * t + 1, pair : pair + TILE, :]
            if k % 2 == 0:
                b = pltpu.roll(b, 4, 0)
            else:
                a = pltpu.roll(a, 4, 0)
            planes[NDEV + p] = jnp.where(sub_low, a, b)
        at = slice(TILE * t, TILE * (t + 1))
        inflow = planes[SENT.index(16)]
        parts = [pltpu.roll(planes[i], LANES - 3 + n, 1) for n, i in enumerate(CARRIERS)]
        tail = jnp.where(place == 0, parts[0], jnp.where(place == 1, parts[1], parts[2]))
        buf[k, TAIL, at, :] = jnp.where(top, inflow, tail)
        for n, i in enumerate(SENT):
            value = planes[n]
            if i in CARRIERS:
                value = jnp.where(top, inflow * (WEIGHTS[i] / WEIGHTS[16]), value)
            buf[k, i, at, :] = value

    copies = [pltpu.make_async_copy(buf.at[k], out_hbm.at[0, k], sem.at[k]) for k in range(CAP)]
    for k in range(CAP):
        for t in range(4):
            slot(k, t)
        copies[k].start()
    for copy in copies:
        copy.wait()


def restore(arrived):
    return pl.pallas_call(
        restore_kernel,
        in_specs=[VMEM_SPEC],
        out_specs=HBM_SPEC,
        out_shape=jax.ShapeDtypeStruct((1, CAP, Q, B, LANES), f32),
        scratch_shapes=[pltpu.VMEM((CAP, Q, B, LANES), f32), pltpu.SemaphoreType.DMA((CAP,))],
        compiler_params=params(),
        name="restore",
    )(arrived)


def block_codes():
    codes = []
    for b in range(NDEV * BLK):
        s, j = divmod(b, BLK)
        after = (s + 1) % NDEV if j % BXD == BXD - 1 else s
        codes.append(s + (j << 4) + (after << 8))
    return np.array(codes, np.int32)


def tables(owner, gy):
    flat = lax.dynamic_index_in_dim(owner, gy, 0, keepdims=False).reshape(-1)
    number = jnp.arange(NDEV * BLK)
    same = (flat[:, None] == flat[None, :]) & (number[None, :] < number[:, None])
    slot = jnp.sum(same.astype(i32), axis=1)
    target = jnp.where(flat >= 0, flat * CAP + slot, -1)
    hit = target[:, None] == jnp.arange(NDEV * CAP)[None, :]
    return jnp.max(jnp.where(hit, block_codes()[:, None], -1), axis=0).astype(i32)


def local(populations, heights, wall_class, wetting, owner):
    gy = lax.axis_index("gy")
    n_gy = lax.axis_size("gy")
    left = lax.ppermute(pack_cols(populations), "gx", [(i, (i + 1) % NDEV) for i in range(NDEV)])
    own, gas, packed, up, down = own_part(
        owner.transpose(2, 0, 1), wetting, populations, heights, wall_class
    )
    up, down = pack_rows(up, down, left)
    up, owner = lax.optimization_barrier((up, owner))
    below = lax.ppermute(up, "gy", [(i, (i - 1) % n_gy) for i in range(n_gy)])
    above = lax.ppermute(down, "gy", [(i, (i + 1) % n_gy) for i in range(n_gy)])
    table = tables(owner, gy)
    post, two, halves, part = inner_part(own, gas, packed, left)
    message = edge_part(part, halves, own, post, two, gas, below, above)
    message, table = lax.optimization_barrier((message, table))
    gathered = lax.all_to_all(message, "gx", split_axis=0, concat_axis=0, tiled=True)
    chosen = sort_blocks(table, gathered)
    arrived = lax.all_to_all(chosen, "gx", split_axis=0, concat_axis=0, tiled=True)
    return restore(arrived)


def solution(mesh):
    return jax.shard_map(
        local,
        mesh=mesh,
        in_specs=(P(None, "gy", "gx"), P(), P(), P(), P()),
        out_specs=P("gy", "gx", None, None, None),
        check_vma=False,
    )
```

```python
import functools

import jax
import jax.numpy as jnp
import numpy as np
from jax import lax
from jax.experimental import pallas as pl
from jax.experimental.pallas import tpu as pltpu
from jax.sharding import PartitionSpec as P

B = 32
CZ = 4
BXD = 3
BYD = 2
CAP = 4
NCLS = 4
BLK = BXD * BYD
Q = 19
TILE = 8
LANES = 128
ROWS = 64
GROUPS = ROWS // TILE
SENT = [i for i in range(Q) if i != 17]
TAIL = 17
NDEV = 16
PIECE = BLK * (B + 4)
SLOTS = CAP * (B + 4)

VELOCITY = [
    (0, 0, 0),
    (1, 0, 0),
    (-1, 0, 0),
    (0, 1, 0),
    (0, -1, 0),
    (0, 0, 1),
    (0, 0, -1),
    (1, 1, 0),
    (-1, -1, 0),
    (1, -1, 0),
    (-1, 1, 0),
    (1, 0, 1),
    (-1, 0, -1),
    (1, 0, -1),
    (-1, 0, 1),
    (0, 1, 1),
    (0, -1, -1),
    (0, 1, -1),
    (0, -1, 1),
]
WEIGHTS = [1.0 / 3.0] + [1.0 / 18.0] * 6 + [1.0 / 36.0] * 12
OPPOSITE = [0, 2, 1, 4, 3, 6, 5, 8, 7, 10, 9, 12, 11, 14, 13, 16, 15, 18, 17]
CARRIERS = (6, 12, 13)

f32 = jnp.float32
i32 = jnp.int32
MIB = 1024 * 1024
PACK_LIMIT = 52 * MIB
OWN_LIMIT = 50 * MIB


def params(limit=16 * MIB):
    return pltpu.CompilerParams(vmem_limit_bytes=limit)


VMEM_SPEC = pl.BlockSpec(memory_space=pltpu.VMEM)
HBM_SPEC = pl.BlockSpec(memory_space=pltpu.HBM)
SMEM_SPEC = pl.BlockSpec(memory_space=pltpu.SMEM)
OWN_SHAPE = jax.ShapeDtypeStruct((Q, 3, ROWS, LANES), f32)
TWO_SHAPE = jax.ShapeDtypeStruct((Q, 4, ROWS, LANES), f32)
LEFT_SHAPE = jax.ShapeDtypeStruct((Q, ROWS, LANES), f32)
EDGE_SHAPE = jax.ShapeDtypeStruct((2 * Q + 2, 4 * LANES), f32)
MESSAGE_SHAPE = jax.ShapeDtypeStruct((NDEV, PIECE, LANES), f32)
PART_SHAPE = jax.ShapeDtypeStruct((NDEV, BLK * 2 * TILE, LANES), f32)
HALVES_SHAPE = jax.ShapeDtypeStruct((NDEV, 4 * BLK, LANES), f32)


def lane_of():
    return lax.broadcasted_iota(i32, (TILE, LANES), 1)


def row_of():
    return lax.broadcasted_iota(i32, (TILE, LANES), 0)


def collide(f, gas):
    pairs = [(i, i + 1) for i in range(1, Q, 2)]
    total = {i: f[i] + f[o] for i, o in pairs}
    diff = {i: f[i] - f[o] for i, o in pairs}
    rho = f[0]
    for i, _ in pairs:
        rho = rho + total[i]
    jx = diff[1] + diff[7] + diff[9] + diff[11] + diff[13]
    jy = diff[3] + diff[7] - diff[9] + diff[15] + diff[17]
    jz = diff[5] + diff[11] - diff[13] + diff[15] - diff[17]
    inv = 1.0 / rho
    scaled = rho - 1.5 * inv * (jx * jx + jy * jy + jz * jz)
    along = {
        1: jx,
        3: jy,
        5: jz,
        7: jx + jy,
        9: jx - jy,
        11: jx + jz,
        13: jx - jz,
        15: jy + jz,
        17: jy - jz,
    }
    is_gas = gas > 0
    out = [None] * Q
    out[0] = jnp.where(
        is_gas, WEIGHTS[0] * gas, -0.6 * f[0] + (1.6 * WEIGHTS[0]) * scaled
    )
    for first, last in ((1, 5), (7, 17)):
        w = WEIGHTS[first]
        base = (1.6 * w) * scaled
        bend = (7.2 * w) * inv
        held = w * gas
        for i in range(first, last + 1, 2):
            cj = along[i]
            even = base + bend * (cj * cj) - 0.3 * total[i]
            odd = 0.25 * diff[i] + (1.5 * w) * cj
            out[i] = jnp.where(is_gas, held, even + odd)
            out[i + 1] = jnp.where(is_gas, held, even - odd)
    return out


def shifted(load, c, shift, lane):
    if shift == 0:
        return load(c)
    here = load(c)
    if shift > 0:
        if c != 3:
            here = jnp.where(lane >= LANES - shift, load((c + 3) % 4), here)
        return pltpu.roll(here, shift, 1)
    if c != 2:
        here = jnp.where(lane < -shift, load((c + 1) % 4), here)
    return pltpu.roll(here, LANES + shift, 1)


def shifted_message(load, c, shift, lane):
    if c != 2:
        return shifted(load, c, shift, lane)
    if shift == 0:
        return jnp.where(lane >= LANES - 8, load(3), load(2))
    if shift > 0:
        here = jnp.where(lane >= LANES - 8 - shift, load(3), load(2))
        here = jnp.where(lane >= LANES - shift, load(1), here)
        return pltpu.roll(here, shift, 1)
    here = jnp.where(lane >= LANES - 8 - shift, load(3), load(2))
    here = jnp.where(lane < -shift, load(0), here)
    return pltpu.roll(here, LANES + shift, 1)


def pull(load, i, c, lane, move=shifted):
    cx, cy, cz = VELOCITY[i]
    moved = move(lambda t: load(i, t, cy), c, 4 * cx + cz, lane)
    if cz == 1:
        wall = move(lambda t: load(OPPOSITE[i], t, 0), c, 0, lane)
        moved = jnp.where(lane % CZ == 0, wall, moved)
    elif cz == -1:
        moved = jnp.where(lane % CZ == CZ - 1, jnp.float32(WEIGHTS[i]), moved)
    return moved


def pack_cols_kernel(pop_hbm, out_ref, buf, sem):
    copies = []
    for g in range(GROUPS):
        rows = pl.ds(TILE * g, TILE)
        copies.append(
            pltpu.make_async_copy(
                pop_hbm.at[:, rows, pl.ds(2 * LANES, LANES)], buf.at[:, rows, :], sem.at[g]
            )
        )
        copies[-1].start()
    lane = lane_of()
    for copy in copies:
        copy.wait()
    for i in range(Q):
        packed = pltpu.roll(buf[i, 0:TILE, :], 16, 1)
        for g in range(1, GROUPS):
            last = buf[i, TILE * g : TILE * (g + 1), :]
            if g < GROUPS - 1:
                last = pltpu.roll(last, 16 * (g + 1), 1)
            packed = jnp.where(lane >= 16 * g, last, packed)
        out_ref[i] = packed


def pack_cols(populations):
    return pl.pallas_call(
        pack_cols_kernel,
        in_specs=[HBM_SPEC],
        out_specs=VMEM_SPEC,
        out_shape=jax.ShapeDtypeStruct((Q, TILE, LANES), f32),
        scratch_shapes=[pltpu.VMEM((Q, ROWS, LANES), f32), pltpu.SemaphoreType.DMA((GROUPS,))],
        compiler_params=params(PACK_LIMIT),
        name="pack_cols",
    )(populations)


def own_kernel(
    owner_ref,
    wet_ref,
    pop_hbm,
    height_hbm,
    kind_hbm,
    post_ref,
    gas_ref,
    packed_ref,
    up_ref,
    down_ref,
    pop,
    height,
    kind,
    pop_sem,
    field_sem,
):
    gy, gx = (lax.axis_index("gy"), lax.axis_index("gx"))
    n_gy = height_hbm.shape[1] // ROWS
    n_x = height_hbm.shape[2] // LANES
    start = lax.rem(gx * (BXD * B) + n_x * LANES - 4, n_x * LANES)
    first = start // LANES
    offset = start - first * LANES
    second = lax.rem(first + 1, n_x)
    up_gy, down_gy = (lax.rem(gy + n_gy - 1, n_gy), lax.rem(gy + 1, n_gy))
    copies = []
    for half, col in enumerate((first, second)):
        cols = pl.ds(pl.multiple_of(col * LANES, LANES), LANES)
        to = pl.ds(LANES * half, LANES)
        for row, at, count in (
            (gy * ROWS, TILE, ROWS),
            (up_gy * ROWS + ROWS - TILE, 0, TILE),
            (down_gy * ROWS, TILE + ROWS, TILE),
        ):
            rows = pl.ds(pl.multiple_of(row, TILE), count)
            n = len(copies)
            copies.append(
                pltpu.make_async_copy(
                    height_hbm.at[:, rows, cols], height.at[:, pl.ds(at, count), to], field_sem.at[n]
                )
            )
            copies.append(
                pltpu.make_async_copy(
                    kind_hbm.at[rows, cols], kind.at[pl.ds(at, count), to], field_sem.at[n + 1]
                )
            )
    for copy in copies:
        copy.start()

    def pop_copy(g):
        rows = pl.ds(pl.multiple_of(TILE * g, TILE), TILE)
        return pltpu.make_async_copy(pop_hbm.at[:, rows, :], pop.at[:, rows, :], pop_sem.at[g])

    for g in range(GROUPS):
        pop_copy(g).start()

    wide = 4 * LANES
    cell = lax.broadcasted_iota(i32, (2 * LANES, wide), 0)
    place = lax.broadcasted_iota(i32, (2 * LANES, wide), 1)
    spread = (cell == offset + 4 + place // CZ - jnp.where(place >= 3 * LANES, LANES, 0)).astype(f32)

    def widen(values):
        return jnp.dot(values.astype(f32), spread, preferred_element_type=f32)

    def active(row, col, j):
        return (owner_ref[j, row, col] >= 0).astype(f32)

    left_gx = lax.rem(gx + NDEV - 1, NDEV)

    def act_tile(row, by, c):
        return active(row, gx, BXD * by + c) if c < 3 else active(row, left_gx, BXD * by + 2)

    for copy in copies:
        copy.wait()
    kinds = widen(kind[...])
    value = wet_ref[0]
    for n in range(1, NCLS):
        value = jnp.where(kinds > n - 0.5, wet_ref[n], value)
    level = 1.0 + value
    lane = lane_of()
    depth = (lane % CZ).astype(f32)
    sub_low = row_of() < 4
    low, high = (TILE + ROWS, 0)
    for s in range(2):
        tall = widen(height[s])
        for c in range(4):
            cols = slice(LANES * c, LANES * (c + 1))
            for by in range(BYD):
                act = act_tile(gy, by, c)
                for rr in range(4):
                    g = 4 * by + rr
                    rows = slice(TILE * (g + 1), TILE * (g + 2))
                    fluid = depth < tall[rows, cols] * act
                    gas_ref[s, g, c] = jnp.where(fluid, 0.0, level[rows, cols])
            act = jnp.where(sub_low, act_tile(down_gy, 0, c), act_tile(up_gy, 1, c))
            here = jnp.where(sub_low, tall[low : low + TILE, cols], tall[high : high + TILE, cols])
            wall = jnp.where(sub_low, level[low : low + TILE, cols], level[high : high + TILE, cols])
            gas_ref[s, GROUPS, c] = jnp.where(depth < here * act, 0.0, wall)
    packed = pltpu.roll(gas_ref[0, 0, 3], 16, 1)
    for g in range(1, GROUPS):
        tile = gas_ref[0, g, 3]
        if g < GROUPS - 1:
            tile = pltpu.roll(tile, 16 * (g + 1), 1)
        packed = jnp.where(lane >= 16 * g, tile, packed)
    packed_ref[...] = packed

    def step(g, carry):
        pop_copy(g).wait()
        rows = pl.ds(pl.multiple_of(TILE * g, TILE), TILE)
        for c in range(3):
            f = [pop[i, rows, LANES * c : LANES * (c + 1)] for i in range(Q)]
            out = collide(f, gas_ref[0, g, c])
            for i in range(Q):
                post_ref[i, c, rows, :] = out[i]
        return carry

    lax.fori_loop(0, GROUPS, step, 0)
    for i in range(Q):
        up_ref[2 * i : 2 * i + 2, :] = pop[i, 0:2, :]
        down_ref[2 * i : 2 * i + 2, :] = pop[i, ROWS - 2 : ROWS, :]


def own_part(owner, wetting, populations, heights, wall_class):
    return pl.pallas_call(
        own_kernel,
        in_specs=[SMEM_SPEC, SMEM_SPEC, HBM_SPEC, HBM_SPEC, HBM_SPEC],
        out_specs=[VMEM_SPEC] * 5,
        out_shape=[
            OWN_SHAPE,
            jax.ShapeDtypeStruct((2, GROUPS + 1, 4, TILE, LANES), f32),
            jax.ShapeDtypeStruct((TILE, LANES), f32),
            jax.ShapeDtypeStruct((2 * Q + 2, 3 * LANES), f32),
            jax.ShapeDtypeStruct((2 * Q + 2, 3 * LANES), f32),
        ],
        scratch_shapes=[
            pltpu.VMEM((Q, ROWS, 3 * LANES), f32),
            pltpu.VMEM((2, ROWS + 2 * TILE, 2 * LANES), i32),
            pltpu.VMEM((ROWS + 2 * TILE, 2 * LANES), i32),
            pltpu.SemaphoreType.DMA((GROUPS,)),
            pltpu.SemaphoreType.DMA((12,)),
        ],
        compiler_params=params(OWN_LIMIT),
        cost_estimate=pl.CostEstimate(flops=8_000_000, bytes_accessed=8_000_000, transcendentals=0),
        name="own_cells",
    )(owner, wetting, populations, heights, wall_class)


def pack_rows_kernel(up_in, down_in, left_ref, up_ref, down_ref):
    up_ref[:, 0 : 3 * LANES] = up_in[...]
    down_ref[:, 0 : 3 * LANES] = down_in[...]
    for i in range(Q):
        first = pltpu.roll(left_ref[i], LANES - 16, 1)
        up_ref[2 * i : 2 * i + 2, 3 * LANES :] = first[0:2]
        down_ref[2 * i : 2 * i + 2, 3 * LANES :] = left_ref[i, TILE - 2 : TILE, :]


def pack_rows(up, down, left):
    return pl.pallas_call(
        pack_rows_kernel,
        in_specs=[VMEM_SPEC] * 3,
        out_specs=[VMEM_SPEC] * 2,
        out_shape=[EDGE_SHAPE, EDGE_SHAPE],
        compiler_params=params(),
        name="pack_rows",
    )(up, down, left)


def store_running(load, out_ref, halves_ref, halves_at, by, rr, lane, start):
    for c in range(3):
        j = BXD * by + c
        tail = pull(load, TAIL, c, lane, shifted_message)
        for n, i in enumerate(SENT):
            value = pull(load, i, c, lane, shifted_message)
            if i in CARRIERS:
                back = 3 - CARRIERS.index(i)
                value = jnp.where(lane % CZ == CZ - 1, pltpu.roll(tail, back, 1), value)
            if n < NDEV:
                at = start(j) + TILE * (rr % 2)
                out_ref[n, at : at + TILE, :] = value
            else:
                m = 8 * (n - NDEV) + 2 * rr
                at = halves_at + 4 * j
                halves_ref[m, at : at + 4, :] = value[0:4]
                halves_ref[m + 1, at : at + 4, :] = value[4:8]


INNER = ((0, 2), (0, 3), (1, 0), (1, 1))
OUTER = ((0, 0), (0, 1), (1, 2), (1, 3))


def inner_kernel(own_ref, gas_ref, packed_ref, left_ref, post_ref, two_ref, halves_ref, part_ref):
    lane = lane_of()
    out = collide([left_ref[i] for i in range(Q)], packed_ref[...])
    for i in range(Q):
        for g in range(GROUPS):
            tile = out[i] if g == GROUPS - 1 else pltpu.roll(out[i], LANES - 16 * (g + 1), 1)
            post_ref[i, TILE * g : TILE * (g + 1), :] = tile

    def second(g, carry):
        def load(i, c, dy):
            rows = pl.ds(TILE * g - dy, TILE)
            return own_ref[i, c, rows, :] if c < 3 else post_ref[i, rows, :]

        for c in range(4):
            out = collide([pull(load, i, c, lane) for i in range(Q)], gas_ref[1, g, c])
            for i in range(Q):
                two_ref[i, c, pl.ds(pl.multiple_of(TILE * g, TILE), TILE), :] = out[i]
        return carry

    lax.fori_loop(1, GROUPS - 1, second, 0)
    for by, rr in INNER:
        at = TILE * (4 * by + rr)
        store_running(
            lambda i, c, dy: two_ref[i, c, at - dy : at - dy + TILE, :],
            part_ref,
            halves_ref,
            0,
            by,
            rr,
            lane,
            lambda j: 2 * TILE * j,
        )


def inner_part(own, gas, packed, left):
    return pl.pallas_call(
        inner_kernel,
        in_specs=[VMEM_SPEC] * 4,
        out_specs=[VMEM_SPEC] * 4,
        out_shape=[LEFT_SHAPE, TWO_SHAPE, HALVES_SHAPE, PART_SHAPE],
        compiler_params=params(),
        cost_estimate=pl.CostEstimate(flops=8_000_000, bytes_accessed=8_000_000, transcendentals=0),
        name="inner_rows",
    )(own, gas, packed, left)


def edge_kernel(
    part_ref,
    halves_ref,
    own_ref,
    post_ref,
    two_ref,
    gas_ref,
    below_ref,
    above_ref,
    out_ref,
    halo,
    top,
    bottom,
    top_two,
    bottom_two,
):
    lane = lane_of()
    sub_low = row_of() < 4
    tall = ROWS - TILE

    out_ref[:, BLK * B :, :] = halves_ref[...]
    for j in range(BLK):
        at = B * j + (2 * TILE if j < BXD else 0)
        out_ref[:, at : at + 2 * TILE, :] = part_ref[:, 2 * TILE * j : 2 * TILE * (j + 1), :]
    halo[...] = jnp.ones(halo.shape, f32)
    for i in range(Q):
        for c in range(4):
            cols = slice(LANES * c, LANES * (c + 1))
            halo[i, c, 0:2, :] = below_ref[2 * i : 2 * i + 2, cols]
            halo[i, c, TILE - 2 : TILE, :] = above_ref[2 * i : 2 * i + 2, cols]
            first = own_ref[i, c, 0:TILE, :] if c < 3 else post_ref[i, 0:TILE, :]
            last = own_ref[i, c, tall:ROWS, :] if c < 3 else post_ref[i, tall:ROWS, :]
            top[i, c, 16:24, :] = first
            bottom[i, c, 8:16, :] = last
            top_two[i, c, 24:32, :] = two_ref[i, c, TILE : 2 * TILE, :]
            bottom_two[i, c, 8:16, :] = two_ref[i, c, tall - TILE : tall, :]
    for c in range(4):
        out = collide([halo[i, c] for i in range(Q)], gas_ref[0, GROUPS, c])
        for i in range(Q):
            top[i, c, 8:16, :] = out[i]
            bottom[i, c, 16:24, :] = out[i]

    def load_first(i, c, dy):
        if dy == 1:
            return top[i, c, 15:23, :]
        return own_ref[i, c, -dy : TILE - dy, :] if c < 3 else post_ref[i, -dy : TILE - dy, :]

    def load_last(i, c, dy):
        if dy == -1:
            return bottom[i, c, 9:17, :]
        return own_ref[i, c, tall - dy : ROWS - dy, :] if c < 3 else post_ref[i, tall - dy : ROWS - dy, :]

    def load_halo(i, c, dy):
        return jnp.where(sub_low, bottom[i, c, 16 - dy : 24 - dy, :], top[i, c, 8 - dy : 16 - dy, :])

    for c in range(4):
        out = collide([pull(load_first, i, c, lane) for i in range(Q)], gas_ref[1, 0, c])
        for i in range(Q):
            top_two[i, c, 16:24, :] = out[i]
        out = collide([pull(load_last, i, c, lane) for i in range(Q)], gas_ref[1, GROUPS - 1, c])
        for i in range(Q):
            bottom_two[i, c, 16:24, :] = out[i]
        out = collide([pull(load_halo, i, c, lane) for i in range(Q)], gas_ref[1, GROUPS, c])
        for i in range(Q):
            top_two[i, c, 8:16, :] = out[i]
            bottom_two[i, c, 24:32, :] = out[i]

    for by, rr in OUTER:
        g = 4 * by + rr

        def load(i, c, dy):
            if by == 0 and (g == 0 or dy == 1):
                return top_two[i, c, 16 + TILE * g - dy : 24 + TILE * g - dy, :]
            if by == 1 and (g == GROUPS - 1 or dy == -1):
                at = TILE * (g - GROUPS + 3) - dy
                return bottom_two[i, c, at : at + TILE, :]
            return two_ref[i, c, TILE * g - dy : TILE * (g + 1) - dy, :]

        store_running(
            load, out_ref, out_ref, BLK * B, by, rr, lane, lambda j: B * j + 2 * TILE * (rr // 2)
        )


def edge_part(part, halves, own, post, two, gas, below, above):
    return pl.pallas_call(
        edge_kernel,
        in_specs=[VMEM_SPEC] * 8,
        out_specs=VMEM_SPEC,
        out_shape=MESSAGE_SHAPE,
        scratch_shapes=[
            pltpu.VMEM((Q, 4, TILE, LANES), f32),
            pltpu.VMEM((Q, 4, 3 * TILE, LANES), f32),
            pltpu.VMEM((Q, 4, 4 * TILE, LANES), f32),
            pltpu.VMEM((Q, 4, 4 * TILE, LANES), f32),
            pltpu.VMEM((Q, 4, 4 * TILE, LANES), f32),
        ],
        compiler_params=params(),
        cost_estimate=pl.CostEstimate(flops=8_000_000, bytes_accessed=8_000_000, transcendentals=0),
        name="edge_rows",
    )(part, halves, own, post, two, gas, below, above)


def sort_kernel(table_ref, in_ref, out_ref):
    lane = lane_of()
    sub_low = row_of() < 4

    def receiver(d, carry):
        halves = []
        for k in range(CAP):
            code = table_ref[d * CAP + k]
            valid = code >= 0
            code = jnp.maximum(code, 0)
            s, j, after_s = (code & 15, (code >> 4) & 7, code >> 8)
            for t in range(4):
                rows = pl.ds(pl.multiple_of(B * j + TILE * t, TILE), TILE)
                tile = jnp.where(lane >= LANES - 8, in_ref[after_s, rows, :], in_ref[s, rows, :])
                out_ref[d, B * k + TILE * t : B * k + TILE * (t + 1), :] = jnp.where(valid, tile, 0.0)
            pair = lax.shift_right_logical(j, 1)
            rows = pl.ds(pl.multiple_of(BLK * B + TILE * pair, TILE), TILE)
            tile = jnp.where(lane >= LANES - 8, in_ref[after_s, rows, :], in_ref[s, rows, :])
            tile = jnp.where(j - 2 * pair == k % 2, tile, pltpu.roll(tile, 4, 0))
            halves.append(jnp.where(valid, tile, 0.0))
        for pair in range(CAP // 2):
            at = CAP * B + TILE * pair
            out_ref[d, at : at + TILE, :] = jnp.where(sub_low, halves[2 * pair], halves[2 * pair + 1])
        return carry

    lax.fori_loop(0, NDEV, receiver, 0, unroll=NDEV)


def sort_blocks(table, arrived):
    return pl.pallas_call(
        sort_kernel,
        in_specs=[SMEM_SPEC, VMEM_SPEC],
        out_specs=VMEM_SPEC,
        out_shape=jax.ShapeDtypeStruct((NDEV, SLOTS, LANES), f32),
        compiler_params=params(),
        name="sort_blocks",
    )(table, arrived)


def restore_kernel(in_ref, out_hbm, buf, sem):
    lane = lane_of()
    sub_low = row_of() < 4
    top = lane % CZ == CZ - 1
    place = lane % CZ

    def slot(k, t):
        rows = slice(B * k + TILE * t, B * k + TILE * (t + 1))
        planes = {m: in_ref[m, rows, :] for m in range(NDEV)}
        pair = CAP * B + TILE * (k // 2)
        for p in range(2):
            a = in_ref[8 * p + 2 * t, pair : pair + TILE, :]
            b = in_ref[8 * p + 2 * t + 1, pair : pair + TILE, :]
            if k % 2 == 0:
                b = pltpu.roll(b, 4, 0)
            else:
                a = pltpu.roll(a, 4, 0)
            planes[NDEV + p] = jnp.where(sub_low, a, b)
        at = slice(TILE * t, TILE * (t + 1))
        inflow = planes[SENT.index(16)]
        parts = [pltpu.roll(planes[i], LANES - 3 + n, 1) for n, i in enumerate(CARRIERS)]
        tail = jnp.where(place == 0, parts[0], jnp.where(place == 1, parts[1], parts[2]))
        buf[k, TAIL, at, :] = jnp.where(top, inflow, tail)
        for n, i in enumerate(SENT):
            value = planes[n]
            if i in CARRIERS:
                value = jnp.where(top, inflow * (WEIGHTS[i] / WEIGHTS[16]), value)
            buf[k, i, at, :] = value

    copies = [pltpu.make_async_copy(buf.at[k], out_hbm.at[0, k], sem.at[k]) for k in range(CAP)]
    for k in range(CAP):
        for t in range(4):
            slot(k, t)
        copies[k].start()
    for copy in copies:
        copy.wait()


def restore(arrived):
    return pl.pallas_call(
        restore_kernel,
        in_specs=[VMEM_SPEC],
        out_specs=HBM_SPEC,
        out_shape=jax.ShapeDtypeStruct((1, CAP, Q, B, LANES), f32),
        scratch_shapes=[pltpu.VMEM((CAP, Q, B, LANES), f32), pltpu.SemaphoreType.DMA((CAP,))],
        compiler_params=params(),
        name="restore",
    )(arrived)


def block_codes():
    codes = []
    for b in range(NDEV * BLK):
        s, j = divmod(b, BLK)
        after = (s + 1) % NDEV if j % BXD == BXD - 1 else s
        codes.append(s + (j << 4) + (after << 8))
    return np.array(codes, np.int32)


def tables(owner, gy):
    flat = lax.dynamic_index_in_dim(owner, gy, 0, keepdims=False).reshape(-1)
    number = jnp.arange(NDEV * BLK)
    same = (flat[:, None] == flat[None, :]) & (number[None, :] < number[:, None])
    slot = jnp.sum(same.astype(i32), axis=1)
    target = jnp.where(flat >= 0, flat * CAP + slot, -1)
    hit = target[:, None] == jnp.arange(NDEV * CAP)[None, :]
    return jnp.max(jnp.where(hit, block_codes()[:, None], -1), axis=0).astype(i32)


def local(populations, heights, wall_class, wetting, owner):
    gy = lax.axis_index("gy")
    n_gy = lax.axis_size("gy")
    left = lax.ppermute(pack_cols(populations), "gx", [(i, (i + 1) % NDEV) for i in range(NDEV)])
    own, gas, packed, up, down = own_part(
        owner.transpose(2, 0, 1), wetting, populations, heights, wall_class
    )
    up, down = pack_rows(up, down, left)
    up, owner = lax.optimization_barrier((up, owner))
    below = lax.ppermute(up, "gy", [(i, (i - 1) % n_gy) for i in range(n_gy)])
    above = lax.ppermute(down, "gy", [(i, (i + 1) % n_gy) for i in range(n_gy)])
    table = tables(owner, gy)
    post, two, halves, part = inner_part(own, gas, packed, left)
    message = edge_part(part, halves, own, post, two, gas, below, above)
    message, table = lax.optimization_barrier((message, table))
    gathered = lax.all_to_all(message, "gx", split_axis=0, concat_axis=0, tiled=True)
    chosen = sort_blocks(table, gathered)
    arrived = lax.all_to_all(chosen, "gx", split_axis=0, concat_axis=0, tiled=True)
    return restore(arrived)


def solution(mesh):
    return jax.shard_map(
        local,
        mesh=mesh,
        in_specs=(P(None, "gy", "gx"), P(), P(), P(), P()),
        out_specs=P("gy", "gx", None, None, None),
        check_vma=False,
    )
```
